32 devices in a mesh: tour: 16 (over z, x, core), feat: 2 (over y).
Axes of the slice: x: 2, y: 2, z: 4, core: 2. Of those that a mesh axis runs over, the one named last changes fastest.
Arguments:
- projected: bfloat16 [8192, 1024], P('tour', 'feat'), may hold values from -220 to 220
- sharpness: float32 [], replicated, may hold values from 5 to 250
- partners: int32 [8, 16], replicated, may hold values from 0 to 15, as said below
- positives: int32 [8192], P('tour'), may hold values from 0 to 8191, as said below
Outputs:
- row_loss: float32 [8192], P('tour')
- view_grad: float32 [8192, 1024], P('tour', 'feat')
The draws below stay inside these ranges and needn't reach their ends.
Inputs may be any that keep to these rules, and one draw needn't show every extreme that they name: For each round r there is one number m_r with partners[r, a] = a XOR m_r for every block a; m_r = M XOR s_r, where M is a nonzero multiple of 8 and s_0, ..., s_7 is an ordering of 0 to 7. positives pairs the views of each block of 512 views among themselves: positives_i lies in i's block, differs from i, and positives of positives_i is i.
All inputs are finite; a program needn't handle non-finite values.
Results may differ from the reference program's by a relative error of at most 0.008.
Values may be sent and summed in bfloat16 or wider, within the bound.
A program may use at most 128 MiB of HBM per device.

```python
import math
import jax
import jax.numpy as jnp
from jax import lax

D = 1024
ROWS_DEV = 512
ROUNDS = 8
BLOCKS = 16
VIEWS = 8192


def draw_projected(key, part):
    key = jax.random.fold_in(key, 11)
    first_key = jax.random.fold_in(key, 0)
    return jnp.clip(jax.random.normal(first_key, (VIEWS, D), jnp.float32), -6.0, 6.0).astype(jnp.bfloat16)


def draw_sharpness(key, part):
    key = jax.random.fold_in(key, 12)
    return jnp.exp(jax.random.uniform(key, (), jnp.float32, math.log(5.0), math.log(20.0)))


def draw_partners(key, part):
    key = jax.random.fold_in(key, 13)
    mask_key, order_key = jax.random.split(key)
    first_mask = 8 * jax.random.randint(mask_key, (), 1, BLOCKS // 8, dtype=jnp.int32)
    low_order = jax.random.permutation(order_key, ROUNDS).astype(jnp.int32)
    round_masks = jnp.bitwise_xor(first_mask, low_order)
    return jnp.bitwise_xor(jnp.arange(BLOCKS, dtype=jnp.int32)[None, :], round_masks[:, None])


def draw_positives(key, part):
    key = jax.random.fold_in(key, 14)
    block_keys = jax.random.split(key, BLOCKS)
    shuffled = jax.vmap(lambda block_key: jax.random.permutation(block_key, ROWS_DEV))(block_keys).astype(jnp.int32)
    swapped = jnp.bitwise_xor(jnp.arange(ROWS_DEV, dtype=jnp.int32), 1)
    block_ids = jnp.arange(BLOCKS, dtype=jnp.int32)[:, None]
    local_pos = jnp.zeros((BLOCKS, ROWS_DEV), jnp.int32).at[block_ids, shuffled].set(shuffled[:, swapped])
    return (local_pos + block_ids * ROWS_DEV).reshape(VIEWS)


def setup_inputs(seed: int = 0) -> dict:
    splits = jax.random.split(jax.random.key(seed), 5)
    projected = draw_projected(jax.random.fold_in(splits[4], 71), 0)
    sharpness = draw_sharpness(jax.random.fold_in(splits[4], 71), 0)
    partners = draw_partners(jax.random.fold_in(splits[4], 71), 0)
    positives = draw_positives(jax.random.fold_in(splits[4], 71), 0)
    return dict(projected=projected, sharpness=sharpness, partners=partners, positives=positives)


EPSILON = 1e-06

def block_scores(block_index, embedded_blocks, partners, sharpness):
    chosen = jnp.concatenate([block_index[None], partners[:, block_index]]).astype(jnp.int32)
    key_blocks = embedded_blocks[chosen].astype(jnp.float32)
    queries = embedded_blocks[block_index].astype(jnp.float32)
    scores = sharpness * jnp.einsum('qd,rkd->rqk', queries, key_blocks, precision=lax.Precision.HIGHEST)
    row_ids = jnp.arange(ROWS_DEV, dtype=jnp.int32)
    self_hit = row_ids[:, None] == row_ids[None, :]
    scores = scores.at[0].set(jnp.where(self_hit, -jnp.inf, scores[0]))
    return (scores, key_blocks, chosen)

def reference(projected, sharpness, partners, positives):
    floats = projected.astype(jnp.float32)
    inverse = lax.rsqrt(lax.optimization_barrier(jnp.sum(floats * floats, -1)) + EPSILON)
    unit_rows = floats * inverse[:, None]
    embedded = unit_rows.astype(jnp.bfloat16)
    embedded_blocks = embedded.reshape(BLOCKS, ROWS_DEV, D)
    starts = jnp.arange(BLOCKS, dtype=jnp.int32) * ROWS_DEV
    local_pos = positives.reshape(BLOCKS, ROWS_DEV) - starts[:, None]
    row_ids = jnp.arange(ROWS_DEV, dtype=jnp.int32)

    def forward_block(block_index):
        scores, key_blocks, chosen = block_scores(block_index, embedded_blocks, partners, sharpness)
        row_peak = lax.optimization_barrier(jnp.max(scores, axis=(0, 2)))
        exp_total = lax.optimization_barrier(jnp.sum(jnp.exp(scores - row_peak[None, :, None]), axis=(0, 2)))
        lse_rows = row_peak + jnp.log(exp_total)
        pos_hit = row_ids[None, :] == local_pos[block_index][:, None]
        loss_rows = lse_rows - lax.optimization_barrier(jnp.sum(jnp.where(pos_hit, scores[0], 0.0), -1))
        return (lse_rows, loss_rows)
    lse_blocks, loss_blocks = lax.map(forward_block, jnp.arange(BLOCKS, dtype=jnp.int32))

    def backward_block(block_index):
        scores, key_blocks, chosen = block_scores(block_index, embedded_blocks, partners, sharpness)
        lse_own = lse_blocks[block_index]
        lse_keys = lse_blocks[chosen]
        pos_hit = (row_ids[None, :] == local_pos[block_index][:, None]).astype(jnp.float32)
        weight = jnp.exp(scores - lse_own[None, :, None]) + jnp.exp(scores - lse_keys[:, None, :])
        weight = weight.at[0].add(-2.0 * pos_hit)
        rounded = lax.optimization_barrier(weight.astype(jnp.bfloat16))
        return sharpness * jnp.einsum('rqk,rkd->qd', rounded.astype(jnp.float32), key_blocks, precision=lax.Precision.HIGHEST)
    unit_grad = lax.map(backward_block, jnp.arange(BLOCKS, dtype=jnp.int32)).reshape(VIEWS, D)
    radial = lax.optimization_barrier(jnp.sum(unit_rows * unit_grad, -1))
    view_grad = inverse[:, None] * (unit_grad - unit_rows * radial[:, None])
    return (loss_blocks.reshape(VIEWS), view_grad)
```

```python
import functools
import math
from functools import reduce

import jax
import jax.numpy as jnp
from jax import lax
from jax.experimental import pallas as pl
from jax.experimental.pallas import tpu as pltpu
from jax.sharding import PartitionSpec as P

EPSILON = 1e-06


def from_partner(value, axis, stride):
    mask = 2**stride
    pairs = [(source, source ^ mask) for source in range(lax.axis_size(axis))]
    return lax.ppermute(value, axis, pairs)


def mask_bit(round_masks, bit_index):
    return jnp.bitwise_and(jnp.right_shift(round_masks, bit_index), 1) == 1


def deliver_each(block, round_masks, bits_count):
    routed = []
    for round_index in range(round_masks.shape[0]):
        moving = block
        for bit_index in range(bits_count):
            arrived = from_partner(moving, "tour", bit_index)
            moving = jnp.where(mask_bit(round_masks[round_index], bit_index), arrived, moving)
        routed.append(moving)
    return routed


def similar(queries, key_block):
    return jnp.einsum("qd,kd->qk", queries, key_block, preferred_element_type=jnp.float32)


def per_device_any(projected, sharpness, partners, positives):
    bits_count = lax.axis_size("tour").bit_length() - 1
    block_index = lax.axis_index("tour")
    row_count = projected.shape[0]
    round_masks = jnp.bitwise_xor(
        lax.dynamic_index_in_dim(partners, block_index, 1, keepdims=False), block_index
    )
    round_count = round_masks.shape[0]
    low_bits = round_count.bit_length() - 1
    high_mask = jnp.left_shift(jnp.right_shift(round_masks[0], low_bits), low_bits)
    code_masks = jnp.bitwise_xor(high_mask, jnp.arange(round_count, dtype=jnp.int32))
    local_pos = positives - block_index * row_count
    floats = projected.astype(jnp.float32)
    inverse = lax.rsqrt(lax.psum(jnp.sum(floats * floats, -1), "feat") + EPSILON)
    unit_rows = floats * inverse[:, None]
    embedded = unit_rows.astype(jnp.bfloat16)
    partner_blocks = deliver_each(embedded, code_masks, bits_count)

    def scored(key_block):
        return lax.psum(similar(embedded, key_block), "feat") * sharpness

    columns = jnp.arange(row_count, dtype=jnp.int32)[None, :]
    query_ids = jnp.arange(embedded.shape[0], dtype=jnp.int32)[:, None]
    own_scores = jnp.where(columns == query_ids, -jnp.inf, scored(embedded))
    all_scores = [own_scores] + [scored(key_block) for key_block in partner_blocks]
    row_peak = reduce(jnp.maximum, [jnp.max(block_scores, -1) for block_scores in all_scores])
    exp_total = reduce(
        jnp.add,
        [jnp.sum(jnp.exp(block_scores - row_peak[:, None]), -1) for block_scores in all_scores],
    )
    lse_rows = row_peak + jnp.log(exp_total)
    pos_hit = columns == local_pos[:, None]
    loss_rows = lse_rows - jnp.sum(jnp.where(pos_hit, own_scores, 0.0), -1)
    stacked = jnp.broadcast_to(lse_rows[None, :], (round_count, row_count))
    for bit_index in range(bits_count):
        arrived = from_partner(stacked, "tour", bit_index)
        stacked = jnp.where(mask_bit(code_masks, bit_index)[:, None], arrived, stacked)
    own_weight = (
        jnp.exp(own_scores - lse_rows[:, None])
        + jnp.exp(own_scores - lse_rows[None, :])
        - 2.0 * pos_hit.astype(jnp.float32)
    )
    unit_grad = jnp.dot(
        own_weight.astype(jnp.bfloat16), embedded, preferred_element_type=jnp.float32
    )
    for round_index in range(len(partner_blocks)):
        block_scores = all_scores[round_index + 1]
        weight = jnp.exp(block_scores - lse_rows[:, None]) + jnp.exp(
            block_scores - stacked[round_index][None, :]
        )
        unit_grad = unit_grad + jnp.dot(
            weight.astype(jnp.bfloat16),
            partner_blocks[round_index],
            preferred_element_type=jnp.float32,
        )
    unit_grad = unit_grad * sharpness
    radial = lax.psum(jnp.sum(unit_rows * unit_grad, -1), "feat")
    view_grad = inverse[:, None] * (unit_grad - unit_rows * radial[:, None])
    return (loss_rows, view_grad)


MESH = pl.DeviceIdType.MESH
LOG2E = math.log2(math.e)
LN2 = math.log(2.0)
GROUP = 8
CHUNKS = 8
FAR = -1e30


def flipped(index, mask):
    bit = 1
    while bit <= mask:
        if mask & bit:
            index = index + bit * (1 - 2 * ((index // bit) % 2))
        bit *= 2
    return index


def log2_add(a, b):
    return jnp.maximum(a, b) + LOG2E * jnp.log(1.0 + jnp.exp2(-jnp.abs(a - b)))


def dot_nt(a, b):
    return lax.dot_general(a, b, (((1,), (1,)), ((), ())), preferred_element_type=jnp.float32)


def dot_tn(a, b):
    return lax.dot_general(a, b, (((0,), (0,)), ((), ())), preferred_element_type=jnp.float32)


def kernel(
    mask, rows, width, sharp_ref, proj_ref, pos_ref, loss_ref, grad_ref,
    raw, q, inv, kb, st, wt, peak, total, spos, lse_own, ex, ex_in, rl, lse_rows, lse_keys,
    g_out, g_in, rad, rad_out, rad_in,
    y_send, y_recv, k_send, k_recv, l_send, l_recv, e_send, e_recv, g_send, g_recv, r_send, r_recv,
):
    half = rows // 2
    step_rows = half // CHUNKS
    t = lax.axis_index("tour")
    f = lax.axis_index("feat")
    other = 1 - f
    peer = (t, other)
    near = {bit: (flipped(t, bit), f) for bit in (1, 2, 4)}
    far = [flipped(t, mask ^ j) for j in range(GROUP)]
    scale = sharp_ref[0, 0] * LOG2E

    barrier = pltpu.get_barrier_semaphore()
    everyone = [peer] + list(near.values()) + [(d, s) for d in far for s in (f, other)]
    for device in everyone:
        pl.semaphore_signal(barrier, inc=1, device_id=device, device_id_type=MESH)
    pl.semaphore_wait(barrier, len(everyone))

    def remote(src, dst, send, recv, device):
        return pltpu.make_async_remote_copy(
            src_ref=src, dst_ref=dst, send_sem=send, recv_sem=recv,
            device_id=device, device_id_type=MESH,
        )

    pieces = 4
    piece = half // pieces

    def y_copy(i):
        if i < pieces:
            spot = pl.ds(pl.multiple_of(other * half + i * piece, piece), piece)
        else:
            spot = pl.ds(pl.multiple_of(f * half, half), half)
        return remote(proj_ref.at[spot], raw.at[f, spot], y_send.at[i], y_recv.at[i], peer)

    for i in range(pieces + 1):
        y_copy(i).start()
    raw[f] = proj_ref[...]

    def normalise(start, count):
        spot = pl.ds(start, count)
        left = raw[0, spot, :].astype(jnp.float32)
        right = raw[1, spot, :].astype(jnp.float32)
        squares = jnp.sum(left * left, -1, keepdims=True) + jnp.sum(right * right, -1, keepdims=True)
        inverse = lax.rsqrt(squares + EPSILON)
        q[0, spot, :] = (left * inverse).astype(jnp.bfloat16)
        q[1, spot, :] = (right * inverse).astype(jnp.bfloat16)
        inv[spot, :] = jnp.broadcast_to(inverse, (count, 128))

    def cross(c):
        spot = pl.ds(pl.multiple_of(f * half + c * step_rows, step_rows), step_rows)
        return remote(q.at[:, spot], kb.at[:, c, 0], k_send.at[0, c], k_recv.at[0, c], (far[0], f))

    def forward(src, dst, bit, c):
        return remote(
            kb.at[:, c, src], kb.at[:, c, dst], k_send.at[dst, c], k_recv.at[dst, c], near[bit]
        )

    hops = {1: (0, 1), 2: (0, 2), 3: (2, 1), 4: (0, 4), 5: (4, 1), 6: (4, 2), 7: (6, 1)}

    def send_key(slot, c):
        if slot == 0:
            return cross(c)
        src, bit = hops[slot]
        return forward(src, slot, bit, c)

    for i in range(pieces):
        y_copy(i).wait_recv()
        normalise(pl.multiple_of(f * half + i * piece, piece), piece)
        for c in range(i * CHUNKS // pieces, (i + 1) * CHUNKS // pieces):
            cross(c).start()

    tile = 128

    def score(c, keys, own):
        for part in range(rows // 256):
            lanes = slice(part * 256, part * 256 + 256)
            block = (dot_nt(keys(0), q[0, lanes, :]) + dot_nt(keys(1), q[1, lanes, :])) * scale
            if own:
                key_ids = lax.broadcasted_iota(jnp.int32, block.shape, 0) + f * half
                query_ids = lax.broadcasted_iota(jnp.int32, block.shape, 1) + part * 256
                block = jnp.where(key_ids == query_ids, FAR, block)
                hit = key_ids == pos_ref[:, lanes]
                spos[:, lanes] = jnp.sum(jnp.where(hit, block, 0.0), 0, keepdims=True)
            for i in range(256 // tile):
                st[part * (256 // tile) + i, c] = block[:, i * tile : (i + 1) * tile]
            folded = block.reshape(half // 8, 8, 256)
            top = jnp.max(folded, 0)
            if own:
                peak[:, lanes] = top
                total[:, lanes] = jnp.sum(jnp.exp2(folded - top[None]), 0)
            else:
                old = peak[:, lanes]
                top = jnp.maximum(top, old)
                peak[:, lanes] = top
                total[:, lanes] = total[:, lanes] * jnp.exp2(old - top) + jnp.sum(
                    jnp.exp2(folded - top[None]), 0
                )

    def own_keys(h):
        return q[h, pl.ds(pl.multiple_of(f * half, half), half), :]

    def chunk_keys(c):
        return lambda h: kb[h, c].reshape(half, width)

    def tick(n):
        @pl.when(n < CHUNKS)
        def _():
            send_key(0, n).wait_recv()
            for slot in (4, 2, 1):
                send_key(slot, n).start()

        @pl.when((n >= 1) & (n < CHUNKS + 1))
        def _():
            send_key(4, n - 1).wait_recv()
            send_key(6, n - 1).start()
            send_key(5, n - 1).start()
            send_key(2, n - 1).wait_recv()
            send_key(3, n - 1).start()

        @pl.when((n >= 2) & (n < CHUNKS + 2))
        def _():
            send_key(6, n - 2).wait_recv()
            send_key(7, n - 2).start()

        @pl.when(n >= 3)
        def _():
            for slot in (1, 3, 5, 7):
                send_key(slot, n - 3).wait_recv()
            score(n - 3, chunk_keys(n - 3), False)

    def tick_body(n, carry):
        tick(n)
        return carry

    lax.fori_loop(0, 2, tick_body, 0)
    y_copy(pieces).wait_recv()
    for i in range(4):
        normalise(pl.multiple_of(other * half + i * (half // 4), half // 4), half // 4)
    score(CHUNKS, own_keys, True)
    lax.fori_loop(2, CHUNKS + 3, tick_body, 0)

    top = jnp.max(peak[...], 0, keepdims=True)
    share = jnp.sum(total[...] * jnp.exp2(peak[...] - top), 0, keepdims=True)
    mine = top + LOG2E * jnp.log(share)
    for h in range(2):
        ex[h] = mine[:, h * half : (h + 1) * half]
        ex[2 + h] = spos[:, h * half : (h + 1) * half]

    def lse_copy(j, h):
        side = f if h == 0 else other
        return remote(ex.at[side], rl.at[j, f], l_send.at[j, h], l_recv.at[j, f], (far[j], side))

    def lse_arrival(j, side):
        return remote(ex.at[0], rl.at[j, side], l_send.at[j, 0], l_recv.at[j, side], peer)

    ex_copy = remote(ex, ex_in, e_send, e_recv, peer)
    for j in range(GROUP - 1, -1, -1):
        for h in range(2):
            lse_copy(j, h).start()
    ex_copy.start()

    ex_copy.wait_recv()
    for h in range(2):
        lanes = slice(h * half, (h + 1) * half)
        lse_own[:, lanes] = log2_add(ex[h], ex_in[h])
        loss_ref[:, lanes] = LN2 * (lse_own[:, lanes] - (ex[2 + h] + ex_in[2 + h]))
    lse_rows[...] = jnp.zeros_like(lse_rows)
    lse_rows[pl.ds(GROUP, 1), :] = log2_add(ex[f], ex_in[f])
    for j in range(GROUP):
        for side in range(2):
            lse_arrival(j, side).wait_recv()
        lse_rows[pl.ds(j, 1), :] = log2_add(rl[j, 0], rl[j, 1])
    columns = lse_rows[...].T
    for j in range(GROUP):
        spread = jnp.broadcast_to(columns[:, j : j + 1], (half, 128))
        lse_keys[pl.ds(0, CHUNKS), j] = spread.reshape(CHUNKS, step_rows, 128)
    lse_keys[CHUNKS] = jnp.broadcast_to(columns[:, GROUP : GROUP + 1], (half, 128)).reshape(
        GROUP, step_rows, 128
    )

    tiles = rows // tile

    def keys_of(c, h):
        if c == CHUNKS:
            return own_keys(h)
        return kb[h, c].reshape(half, width)

    def g_copy(i):
        return remote(g_out.at[i], g_in.at[i], g_send.at[i], g_recv.at[i], peer)

    def send_tile(i, carry):
        lanes = pl.ds(pl.multiple_of(i * tile, tile), tile)
        lse_query = lse_own[:, lanes]
        acc = jnp.zeros((tile, width), jnp.float32)
        inner = jnp.zeros((8, tile), jnp.float32)
        for c in range(CHUNKS + 1):
            block = st[i, c]
            weight = jnp.exp2(block - lse_query) + jnp.exp2(block - lse_keys[c].reshape(half, 128))
            if c == CHUNKS:
                key_ids = lax.broadcasted_iota(jnp.int32, block.shape, 0) + f * half
                weight = weight - jnp.where(key_ids == pos_ref[:, lanes], 2.0, 0.0)
            rounded = weight.astype(jnp.bfloat16)
            wt[i, c] = rounded
            inner = inner + jnp.sum(
                (rounded.astype(jnp.float32) * block).reshape(half // 8, 8, tile), 0
            )
            acc = acc + dot_tn(rounded, keys_of(c, other))
        rad[:, lanes] = jnp.sum(inner, 0, keepdims=True)
        g_out[i] = acc.astype(jnp.bfloat16)
        g_copy(i).start()
        return carry

    lax.fori_loop(0, tiles, send_tile, 0)
    rad_out[0] = rad[...]
    rad_copy = remote(rad_out, rad_in, r_send, r_recv, peer)
    rad_copy.start()

    def keep_tile(i, carry):
        acc = jnp.zeros((tile, width), jnp.float32)
        for c in range(CHUNKS + 1):
            acc = acc + dot_tn(wt[i, c], keys_of(c, f))
        grad_ref[pl.ds(pl.multiple_of(i * tile, tile), tile), :] = acc
        return carry

    lax.fori_loop(0, tiles, keep_tile, 0)
    rad_copy.wait_recv()
    radial = jnp.broadcast_to(LN2 * (rad_out[0] + rad_in[0]), (128, rows)).T
    sharpness = sharp_ref[0, 0]
    for i in range(tiles):
        spot = slice(i * tile, (i + 1) * tile)
        g_copy(i).wait_recv()
        inverse = inv[spot, :1]
        unit = proj_ref[spot, :].astype(jnp.float32) * inverse
        whole = (grad_ref[spot, :] + g_in[i].astype(jnp.float32)) * sharpness
        grad_ref[spot, :] = inverse * (whole - unit * radial[spot, :1])

    for i in range(pieces + 1):
        y_copy(i).wait_send()
    for slot in range(GROUP):
        for c in range(CHUNKS):
            send_key(slot, c).wait_send()
    for j in range(GROUP):
        for h in range(2):
            lse_copy(j, h).wait_send()
    ex_copy.wait_send()
    rad_copy.wait_send()
    for i in range(tiles):
        g_copy(i).wait_send()


def per_device(projected, sharpness, partners, positives):
    rows, width = projected.shape
    blocks = lax.axis_size("tour")
    if blocks != 2 * GROUP or lax.axis_size("feat") != 2:
        return per_device_any(projected, sharpness, partners, positives)
    half = rows // 2
    step_rows = half // CHUNKS
    tiles = rows // 128
    local_pos = (positives - lax.axis_index("tour") * rows)[None, :]
    bf16, f32 = jnp.bfloat16, jnp.float32
    dma = pltpu.SemaphoreType.DMA
    loss, grad = pl.pallas_call(
        functools.partial(kernel, GROUP, rows, width),
        out_shape=(
            jax.ShapeDtypeStruct((1, rows), f32),
            jax.ShapeDtypeStruct((rows, width), f32),
        ),
        in_specs=[
            pl.BlockSpec(memory_space=pltpu.SMEM),
            pl.BlockSpec(memory_space=pltpu.VMEM),
            pl.BlockSpec(memory_space=pltpu.VMEM),
        ],
        out_specs=[pl.BlockSpec(memory_space=pltpu.VMEM)] * 2,
        scratch_shapes=[
            pltpu.VMEM((2, rows, width), bf16),
            pltpu.VMEM((2, rows, width), bf16),
            pltpu.VMEM((rows, 128), f32),
            pltpu.VMEM((2, CHUNKS, GROUP, step_rows, width), bf16),
            pltpu.VMEM((tiles, CHUNKS + 1, half, 128), f32),
            pltpu.VMEM((tiles, CHUNKS + 1, half, 128), bf16),
            pltpu.VMEM((8, rows), f32),
            pltpu.VMEM((8, rows), f32),
            pltpu.VMEM((1, rows), f32),
            pltpu.VMEM((1, rows), f32),
            pltpu.VMEM((4, 1, half), f32),
            pltpu.VMEM((4, 1, half), f32),
            pltpu.VMEM((GROUP, 2, 1, half), f32),
            pltpu.VMEM((128, half), f32),
            pltpu.VMEM((CHUNKS + 1, GROUP, step_rows, 128), f32),
            pltpu.VMEM((tiles, 128, width), bf16),
            pltpu.VMEM((tiles, 128, width), bf16),
            pltpu.VMEM((1, rows), f32),
            pltpu.VMEM((1, 1, rows), f32),
            pltpu.VMEM((1, 1, rows), f32),
            dma((5,)), dma((5,)),
            dma((GROUP, CHUNKS)), dma((GROUP, CHUNKS)),
            dma((GROUP, 2)), dma((GROUP, 2)),
            dma, dma,
            dma((tiles,)), dma((tiles,)),
            dma, dma,
        ],
        compiler_params=pltpu.CompilerParams(
            collective_id=0, has_side_effects=True, vmem_limit_bytes=50 * 1024 * 1024
        ),
        cost_estimate=pl.CostEstimate(
            flops=9 * 4 * rows * half * 2 * width, bytes_accessed=4 * rows * width,
            transcendentals=27 * rows * half,
        ),
    )(sharpness.reshape(1, 1), projected, local_pos)
    return loss[0], grad


def solution(mesh):
    in_specs = (P("tour", "feat"), P(), P(), P("tour"))
    out_specs = (P("tour"), P("tour", "feat"))
    return jax.shard_map(
        per_device, mesh=mesh, in_specs=in_specs, out_specs=out_specs, check_vma=False
    )
```

```python
import functools
import math
from functools import reduce

import jax
import jax.numpy as jnp
from jax import lax
from jax.experimental import pallas as pl
from jax.experimental.pallas import tpu as pltpu
from jax.sharding import PartitionSpec as P

EPSILON = 1e-06


def from_partner(value, axis, stride):
    mask = 2**stride
    pairs = [(source, source ^ mask) for source in range(lax.axis_size(axis))]
    return lax.ppermute(value, axis, pairs)


def mask_bit(round_masks, bit_index):
    return jnp.bitwise_and(jnp.right_shift(round_masks, bit_index), 1) == 1


def deliver_each(block, round_masks, bits_count):
    routed = []
    for round_index in range(round_masks.shape[0]):
        moving = block
        for bit_index in range(bits_count):
            arrived = from_partner(moving, "tour", bit_index)
            moving = jnp.where(mask_bit(round_masks[round_index], bit_index), arrived, moving)
        routed.append(moving)
    return routed


def similar(queries, key_block):
    return jnp.einsum("qd,kd->qk", queries, key_block, preferred_element_type=jnp.float32)


def per_device_any(projected, sharpness, partners, positives):
    bits_count = lax.axis_size("tour").bit_length() - 1
    block_index = lax.axis_index("tour")
    row_count = projected.shape[0]
    round_masks = jnp.bitwise_xor(
        lax.dynamic_index_in_dim(partners, block_index, 1, keepdims=False), block_index
    )
    round_count = round_masks.shape[0]
    low_bits = round_count.bit_length() - 1
    high_mask = jnp.left_shift(jnp.right_shift(round_masks[0], low_bits), low_bits)
    code_masks = jnp.bitwise_xor(high_mask, jnp.arange(round_count, dtype=jnp.int32))
    local_pos = positives - block_index * row_count
    floats = projected.astype(jnp.float32)
    inverse = lax.rsqrt(lax.psum(jnp.sum(floats * floats, -1), "feat") + EPSILON)
    unit_rows = floats * inverse[:, None]
    embedded = unit_rows.astype(jnp.bfloat16)
    partner_blocks = deliver_each(embedded, code_masks, bits_count)

    def scored(key_block):
        return lax.psum(similar(embedded, key_block), "feat") * sharpness

    columns = jnp.arange(row_count, dtype=jnp.int32)[None, :]
    query_ids = jnp.arange(embedded.shape[0], dtype=jnp.int32)[:, None]
    own_scores = jnp.where(columns == query_ids, -jnp.inf, scored(embedded))
    all_scores = [own_scores] + [scored(key_block) for key_block in partner_blocks]
    row_peak = reduce(jnp.maximum, [jnp.max(block_scores, -1) for block_scores in all_scores])
    exp_total = reduce(
        jnp.add,
        [jnp.sum(jnp.exp(block_scores - row_peak[:, None]), -1) for block_scores in all_scores],
    )
    lse_rows = row_peak + jnp.log(exp_total)
    pos_hit = columns == local_pos[:, None]
    loss_rows = lse_rows - jnp.sum(jnp.where(pos_hit, own_scores, 0.0), -1)
    stacked = jnp.broadcast_to(lse_rows[None, :], (round_count, row_count))
    for bit_index in range(bits_count):
        arrived = from_partner(stacked, "tour", bit_index)
        stacked = jnp.where(mask_bit(code_masks, bit_index)[:, None], arrived, stacked)
    own_weight = (
        jnp.exp(own_scores - lse_rows[:, None])
        + jnp.exp(own_scores - lse_rows[None, :])
        - 2.0 * pos_hit.astype(jnp.float32)
    )
    unit_grad = jnp.dot(
        own_weight.astype(jnp.bfloat16), embedded, preferred_element_type=jnp.float32
    )
    for round_index in range(len(partner_blocks)):
        block_scores = all_scores[round_index + 1]
        weight = jnp.exp(block_scores - lse_rows[:, None]) + jnp.exp(
            block_scores - stacked[round_index][None, :]
        )
        unit_grad = unit_grad + jnp.dot(
            weight.astype(jnp.bfloat16),
            partner_blocks[round_index],
            preferred_element_type=jnp.float32,
        )
    unit_grad = unit_grad * sharpness
    radial = lax.psum(jnp.sum(unit_rows * unit_grad, -1), "feat")
    view_grad = inverse[:, None] * (unit_grad - unit_rows * radial[:, None])
    return (loss_rows, view_grad)


MESH = pl.DeviceIdType.MESH
LOG2E = math.log2(math.e)
LN2 = math.log(2.0)
GROUP = 8
CHUNKS = 8
WINDOW = 4
FAR = -1e30


def flipped(index, mask):
    bit = 1
    while bit <= mask:
        if mask & bit:
            index = index + bit * (1 - 2 * ((index // bit) % 2))
        bit *= 2
    return index


def log2_add(a, b):
    return jnp.maximum(a, b) + LOG2E * jnp.log(1.0 + jnp.exp2(-jnp.abs(a - b)))


def dot_nt(a, b):
    return lax.dot_general(a, b, (((1,), (1,)), ((), ())), preferred_element_type=jnp.float32)


def dot_tn(a, b):
    return lax.dot_general(a, b, (((0,), (0,)), ((), ())), preferred_element_type=jnp.float32)


def kernel(
    mask, rows, width, sharp_ref, proj_ref, pos_ref, loss_ref, grad_ref,
    raw, q, inv, kb, st, wt, peak, total, spos, lse_own, ex, ex_in, rl, lse_rows, lse_keys,
    g_out, g_in, rad, rad_out, rad_in,
    own_sem, y_send, y_recv, k_send, k_recv, l_send, l_recv, e_send, e_recv, g_send, g_recv, r_send, r_recv,
):
    half = rows // 2
    step_rows = half // CHUNKS
    t = lax.axis_index("tour")
    f = lax.axis_index("feat")
    other = 1 - f
    peer = (t, other)
    near = {bit: (flipped(t, bit), f) for bit in (1, 2, 4)}
    far = [flipped(t, mask ^ j) for j in range(GROUP)]
    scale = sharp_ref[0, 0] * LOG2E

    barrier = pltpu.get_barrier_semaphore()
    everyone = [peer] + list(near.values()) + [(d, s) for d in far for s in (f, other)]
    for device in everyone:
        pl.semaphore_signal(barrier, inc=1, device_id=device, device_id_type=MESH)
    pl.semaphore_wait(barrier, len(everyone))

    def remote(src, dst, send, recv, device):
        return pltpu.make_async_remote_copy(
            src_ref=src, dst_ref=dst, send_sem=send, recv_sem=recv,
            device_id=device, device_id_type=MESH,
        )

    pieces = 4
    piece = half // pieces

    def y_copy(i):
        side = other if i < pieces else f
        spot = pl.ds(pl.multiple_of(side * half + (i % pieces) * piece, piece), piece)
        return remote(proj_ref.at[spot], raw.at[f, spot], y_send.at[i], y_recv.at[i], peer)

    for i in range(pieces):
        y_copy(i).start()
    own_copy = pltpu.make_async_copy(proj_ref, raw.at[f], own_sem)
    own_copy.start()
    own_copy.wait()

    def normalise(start, count):
        spot = pl.ds(start, count)
        left = raw[0, spot, :].astype(jnp.float32)
        right = raw[1, spot, :].astype(jnp.float32)
        squares = jnp.sum(left * left, -1, keepdims=True) + jnp.sum(right * right, -1, keepdims=True)
        inverse = lax.rsqrt(squares + EPSILON)
        q[0, spot, :] = (left * inverse).astype(jnp.bfloat16)
        q[1, spot, :] = (right * inverse).astype(jnp.bfloat16)
        inv[spot, :] = jnp.broadcast_to(inverse, (count, 128))

    def cross(c):
        spot = pl.ds(pl.multiple_of(f * half + c * step_rows, step_rows), step_rows)
        return remote(q.at[:, spot], kb.at[:, c, 0], k_send.at[0, c], k_recv.at[0, c], (far[0], f))

    def forward(src, dst, bit, c):
        return remote(
            kb.at[:, c, src], kb.at[:, c, dst], k_send.at[dst, c], k_recv.at[dst, c], near[bit]
        )

    hops = {1: (0, 1), 2: (0, 2), 3: (2, 1), 4: (0, 4), 5: (4, 1), 6: (4, 2), 7: (6, 1)}

    def send_key(slot, c):
        if slot == 0:
            return cross(c)
        src, bit = hops[slot]
        return forward(src, slot, bit, c)

    for i in range(pieces):
        y_copy(i).wait_recv()
        normalise(pl.multiple_of(f * half + i * piece, piece), piece)
        for c in range(i * CHUNKS // pieces, (i + 1) * CHUNKS // pieces):
            if c < WINDOW:
                cross(c).start()
        y_copy(pieces + i).start()

    tile = 128

    def score(c, keys, own):
        for part in range(rows // 256):
            lanes = slice(part * 256, part * 256 + 256)
            block = (dot_nt(keys(0), q[0, lanes, :]) + dot_nt(keys(1), q[1, lanes, :])) * scale
            if own:
                key_ids = lax.broadcasted_iota(jnp.int32, block.shape, 0) + f * half
                query_ids = lax.broadcasted_iota(jnp.int32, block.shape, 1) + part * 256
                block = jnp.where(key_ids == query_ids, FAR, block)
                hit = key_ids == pos_ref[:, lanes]
                spos[:, lanes] = jnp.sum(jnp.where(hit, block, 0.0), 0, keepdims=True)
            for i in range(256 // tile):
                st[part * (256 // tile) + i, c] = block[:, i * tile : (i + 1) * tile]
            folded = block.reshape(half // 8, 8, 256)
            top = jnp.max(folded, 0)
            if own:
                peak[:, lanes] = top
                total[:, lanes] = jnp.sum(jnp.exp2(folded - top[None]), 0)
            else:
                old = peak[:, lanes]
                top = jnp.maximum(top, old)
                peak[:, lanes] = top
                total[:, lanes] = total[:, lanes] * jnp.exp2(old - top) + jnp.sum(
                    jnp.exp2(folded - top[None]), 0
                )

    def own_keys(h):
        return q[h, pl.ds(pl.multiple_of(f * half, half), half), :]

    def chunk_keys(c):
        return lambda h: kb[h, c].reshape(half, width)

    def tick(n):
        @pl.when(n < CHUNKS)
        def _():
            send_key(0, n).wait_recv()
            for slot in (4, 2, 1):
                send_key(slot, n).start()

        @pl.when(n + WINDOW < CHUNKS)
        def _():
            cross(n + WINDOW).start()

        @pl.when((n >= 1) & (n < CHUNKS + 1))
        def _():
            send_key(4, n - 1).wait_recv()
            send_key(6, n - 1).start()
            send_key(5, n - 1).start()
            send_key(2, n - 1).wait_recv()
            send_key(3, n - 1).start()

        @pl.when((n >= 2) & (n < CHUNKS + 2))
        def _():
            send_key(6, n - 2).wait_recv()
            send_key(7, n - 2).start()

        @pl.when(n >= 3)
        def _():
            for slot in (1, 3, 5, 7):
                send_key(slot, n - 3).wait_recv()
            score(n - 3, chunk_keys(n - 3), False)

    def tick_body(n, carry):
        tick(n)
        return carry

    lax.fori_loop(0, 2, tick_body, 0)
    for i in range(pieces):
        y_copy(pieces + i).wait_recv()
        normalise(pl.multiple_of(other * half + i * piece, piece), piece)
    score(CHUNKS, own_keys, True)
    lax.fori_loop(2, CHUNKS + 3, tick_body, 0)

    top = jnp.max(peak[...], 0, keepdims=True)
    share = jnp.sum(total[...] * jnp.exp2(peak[...] - top), 0, keepdims=True)
    mine = top + LOG2E * jnp.log(share)
    for h in range(2):
        ex[h] = mine[:, h * half : (h + 1) * half]
        ex[2 + h] = spos[:, h * half : (h + 1) * half]

    def lse_copy(j, h):
        side = f if h == 0 else other
        return remote(ex.at[side], rl.at[j, f], l_send.at[j, h], l_recv.at[j, f], (far[j], side))

    def lse_arrival(j, side):
        return remote(ex.at[0], rl.at[j, side], l_send.at[j, 0], l_recv.at[j, side], peer)

    ex_copy = remote(ex, ex_in, e_send, e_recv, peer)
    for j in range(GROUP - 1, -1, -1):
        for h in range(2):
            lse_copy(j, h).start()
    ex_copy.start()

    ex_copy.wait_recv()
    for h in range(2):
        lanes = slice(h * half, (h + 1) * half)
        lse_own[:, lanes] = log2_add(ex[h], ex_in[h])
        loss_ref[:, lanes] = LN2 * (lse_own[:, lanes] - (ex[2 + h] + ex_in[2 + h]))
    lse_rows[...] = jnp.zeros_like(lse_rows)
    lse_rows[pl.ds(GROUP, 1), :] = log2_add(ex[f], ex_in[f])
    for j in range(GROUP):
        for side in range(2):
            lse_arrival(j, side).wait_recv()
        lse_rows[pl.ds(j, 1), :] = log2_add(rl[j, 0], rl[j, 1])
    columns = lse_rows[...].T
    for j in range(GROUP):
        spread = jnp.broadcast_to(columns[:, j : j + 1], (half, 128))
        lse_keys[pl.ds(0, CHUNKS), j] = spread.reshape(CHUNKS, step_rows, 128)
    lse_keys[CHUNKS] = jnp.broadcast_to(columns[:, GROUP : GROUP + 1], (half, 128)).reshape(
        GROUP, step_rows, 128
    )

    tiles = rows // tile

    def keys_of(c, h):
        if c == CHUNKS:
            return own_keys(h)
        return kb[h, c].reshape(half, width)

    def g_copy(i):
        return remote(g_out.at[i], g_in.at[i], g_send.at[i], g_recv.at[i], peer)

    def send_tile(i, carry):
        lanes = pl.ds(pl.multiple_of(i * tile, tile), tile)
        lse_query = lse_own[:, lanes]
        acc = jnp.zeros((tile, width), jnp.float32)
        inner = jnp.zeros((8, tile), jnp.float32)
        for c in range(CHUNKS + 1):
            block = st[i, c]
            weight = jnp.exp2(block - lse_query) + jnp.exp2(block - lse_keys[c].reshape(half, 128))
            if c == CHUNKS:
                key_ids = lax.broadcasted_iota(jnp.int32, block.shape, 0) + f * half
                weight = weight - jnp.where(key_ids == pos_ref[:, lanes], 2.0, 0.0)
            rounded = weight.astype(jnp.bfloat16)
            wt[i, c] = rounded
            inner = inner + jnp.sum(
                (rounded.astype(jnp.float32) * block).reshape(half // 8, 8, tile), 0
            )
            acc = acc + dot_tn(rounded, keys_of(c, other))
        rad[:, lanes] = jnp.sum(inner, 0, keepdims=True)
        g_out[i] = acc.astype(jnp.bfloat16)
        g_copy(i).start()
        return carry

    lax.fori_loop(0, tiles, send_tile, 0)
    rad_out[0] = rad[...]
    rad_copy = remote(rad_out, rad_in, r_send, r_recv, peer)
    rad_copy.start()

    def keep_tile(i, carry):
        acc = jnp.zeros((tile, width), jnp.float32)
        for c in range(CHUNKS + 1):
            acc = acc + dot_tn(wt[i, c], keys_of(c, f))
        grad_ref[pl.ds(pl.multiple_of(i * tile, tile), tile), :] = acc
        return carry

    lax.fori_loop(0, tiles, keep_tile, 0)
    rad_copy.wait_recv()
    radial = jnp.broadcast_to(LN2 * (rad_out[0] + rad_in[0]), (128, rows)).T
    sharpness = sharp_ref[0, 0]
    for i in range(tiles):
        spot = slice(i * tile, (i + 1) * tile)
        g_copy(i).wait_recv()
        inverse = inv[spot, :1]
        unit = raw[f, spot, :].astype(jnp.float32) * inverse
        whole = (grad_ref[spot, :] + g_in[i].astype(jnp.float32)) * sharpness
        grad_ref[spot, :] = inverse * (whole - unit * radial[spot, :1])

    for i in range(2 * pieces):
        y_copy(i).wait_send()
    for slot in range(GROUP):
        for c in range(CHUNKS):
            send_key(slot, c).wait_send()
    for j in range(GROUP):
        for h in range(2):
            lse_copy(j, h).wait_send()
    ex_copy.wait_send()
    rad_copy.wait_send()
    for i in range(tiles):
        g_copy(i).wait_send()


def per_device(projected, sharpness, partners, positives):
    rows, width = projected.shape
    blocks = lax.axis_size("tour")
    if blocks != 2 * GROUP or lax.axis_size("feat") != 2:
        return per_device_any(projected, sharpness, partners, positives)
    half = rows // 2
    step_rows = half // CHUNKS
    tiles = rows // 128
    local_pos = (positives - lax.axis_index("tour") * rows)[None, :]
    bf16, f32 = jnp.bfloat16, jnp.float32
    dma = pltpu.SemaphoreType.DMA
    loss, grad = pl.pallas_call(
        functools.partial(kernel, GROUP, rows, width),
        out_shape=(
            jax.ShapeDtypeStruct((1, rows), f32),
            jax.ShapeDtypeStruct((rows, width), f32),
        ),
        in_specs=[
            pl.BlockSpec(memory_space=pltpu.SMEM),
            pl.BlockSpec(memory_space=pl.ANY),
            pl.BlockSpec(memory_space=pltpu.VMEM),
        ],
        out_specs=[pl.BlockSpec(memory_space=pltpu.VMEM)] * 2,
        scratch_shapes=[
            pltpu.VMEM((2, rows, width), bf16),
            pltpu.VMEM((2, rows, width), bf16),
            pltpu.VMEM((rows, 128), f32),
            pltpu.VMEM((2, CHUNKS, GROUP, step_rows, width), bf16),
            pltpu.VMEM((tiles, CHUNKS + 1, half, 128), f32),
            pltpu.VMEM((tiles, CHUNKS + 1, half, 128), bf16),
            pltpu.VMEM((8, rows), f32),
            pltpu.VMEM((8, rows), f32),
            pltpu.VMEM((1, rows), f32),
            pltpu.VMEM((1, rows), f32),
            pltpu.VMEM((4, 1, half), f32),
            pltpu.VMEM((4, 1, half), f32),
            pltpu.VMEM((GROUP, 2, 1, half), f32),
            pltpu.VMEM((128, half), f32),
            pltpu.VMEM((CHUNKS + 1, GROUP, step_rows, 128), f32),
            pltpu.VMEM((tiles, 128, width), bf16),
            pltpu.VMEM((tiles, 128, width), bf16),
            pltpu.VMEM((1, rows), f32),
            pltpu.VMEM((1, 1, rows), f32),
            pltpu.VMEM((1, 1, rows), f32),
            dma, dma((8,)), dma((8,)),
            dma((GROUP, CHUNKS)), dma((GROUP, CHUNKS)),
            dma((GROUP, 2)), dma((GROUP, 2)),
            dma, dma,
            dma((tiles,)), dma((tiles,)),
            dma, dma,
        ],
        compiler_params=pltpu.CompilerParams(
            collective_id=0, has_side_effects=True, vmem_limit_bytes=50 * 1024 * 1024
        ),
        cost_estimate=pl.CostEstimate(
            flops=9 * 4 * rows * half * 2 * width, bytes_accessed=4 * rows * width,
            transcendentals=27 * rows * half,
        ),
    )(sharpness.reshape(1, 1), projected, local_pos)
    return loss[0], grad


def solution(mesh):
    in_specs = (P("tour", "feat"), P(), P(), P("tour"))
    out_specs = (P("tour"), P("tour", "feat"))
    return jax.shard_map(
        per_device, mesh=mesh, in_specs=in_specs, out_specs=out_specs, check_vma=False
    )
```

```python
import functools
import math
from functools import reduce

import jax
import jax.numpy as jnp
from jax import lax
from jax.experimental import pallas as pl
from jax.experimental.pallas import tpu as pltpu
from jax.sharding import PartitionSpec as P

EPSILON = 1e-06


def from_partner(value, axis, stride):
    mask = 2**stride
    pairs = [(source, source ^ mask) for source in range(lax.axis_size(axis))]
    return lax.ppermute(value, axis, pairs)


def mask_bit(round_masks, bit_index):
    return jnp.bitwise_and(jnp.right_shift(round_masks, bit_index), 1) == 1


def deliver_each(block, round_masks, bits_count):
    routed = []
    for round_index in range(round_masks.shape[0]):
        moving = block
        for bit_index in range(bits_count):
            arrived = from_partner(moving, "tour", bit_index)
            moving = jnp.where(mask_bit(round_masks[round_index], bit_index), arrived, moving)
        routed.append(moving)
    return routed


def similar(queries, key_block):
    return jnp.einsum("qd,kd->qk", queries, key_block, preferred_element_type=jnp.float32)


def per_device_any(projected, sharpness, partners, positives):
    bits_count = lax.axis_size("tour").bit_length() - 1
    block_index = lax.axis_index("tour")
    row_count = projected.shape[0]
    round_masks = jnp.bitwise_xor(
        lax.dynamic_index_in_dim(partners, block_index, 1, keepdims=False), block_index
    )
    round_count = round_masks.shape[0]
    low_bits = round_count.bit_length() - 1
    high_mask = jnp.left_shift(jnp.right_shift(round_masks[0], low_bits), low_bits)
    code_masks = jnp.bitwise_xor(high_mask, jnp.arange(round_count, dtype=jnp.int32))
    local_pos = positives - block_index * row_count
    floats = projected.astype(jnp.float32)
    inverse = lax.rsqrt(lax.psum(jnp.sum(floats * floats, -1), "feat") + EPSILON)
    unit_rows = floats * inverse[:, None]
    embedded = unit_rows.astype(jnp.bfloat16)
    partner_blocks = deliver_each(embedded, code_masks, bits_count)

    def scored(key_block):
        return lax.psum(similar(embedded, key_block), "feat") * sharpness

    columns = jnp.arange(row_count, dtype=jnp.int32)[None, :]
    query_ids = jnp.arange(embedded.shape[0], dtype=jnp.int32)[:, None]
    own_scores = jnp.where(columns == query_ids, -jnp.inf, scored(embedded))
    all_scores = [own_scores] + [scored(key_block) for key_block in partner_blocks]
    row_peak = reduce(jnp.maximum, [jnp.max(block_scores, -1) for block_scores in all_scores])
    exp_total = reduce(
        jnp.add,
        [jnp.sum(jnp.exp(block_scores - row_peak[:, None]), -1) for block_scores in all_scores],
    )
    lse_rows = row_peak + jnp.log(exp_total)
    pos_hit = columns == local_pos[:, None]
    loss_rows = lse_rows - jnp.sum(jnp.where(pos_hit, own_scores, 0.0), -1)
    stacked = jnp.broadcast_to(lse_rows[None, :], (round_count, row_count))
    for bit_index in range(bits_count):
        arrived = from_partner(stacked, "tour", bit_index)
        stacked = jnp.where(mask_bit(code_masks, bit_index)[:, None], arrived, stacked)
    own_weight = (
        jnp.exp(own_scores - lse_rows[:, None])
        + jnp.exp(own_scores - lse_rows[None, :])
        - 2.0 * pos_hit.astype(jnp.float32)
    )
    unit_grad = jnp.dot(
        own_weight.astype(jnp.bfloat16), embedded, preferred_element_type=jnp.float32
    )
    for round_index in range(len(partner_blocks)):
        block_scores = all_scores[round_index + 1]
        weight = jnp.exp(block_scores - lse_rows[:, None]) + jnp.exp(
            block_scores - stacked[round_index][None, :]
        )
        unit_grad = unit_grad + jnp.dot(
            weight.astype(jnp.bfloat16),
            partner_blocks[round_index],
            preferred_element_type=jnp.float32,
        )
    unit_grad = unit_grad * sharpness
    radial = lax.psum(jnp.sum(unit_rows * unit_grad, -1), "feat")
    view_grad = inverse[:, None] * (unit_grad - unit_rows * radial[:, None])
    return (loss_rows, view_grad)


MESH = pl.DeviceIdType.MESH
LOG2E = math.log2(math.e)
LN2 = math.log(2.0)
GROUP = 8
CHUNKS = 8
STEPS = 16
WINDOW = 4
LAGS = (2, 4, 5)
FAR = -1e30


def flipped(index, mask):
    bit = 1
    while bit <= mask:
        if mask & bit:
            index = index + bit * (1 - 2 * ((index // bit) % 2))
        bit *= 2
    return index


def log2_add(a, b):
    return jnp.maximum(a, b) + LOG2E * jnp.log(1.0 + jnp.exp2(-jnp.abs(a - b)))


def dot_nt(a, b):
    return lax.dot_general(a, b, (((1,), (1,)), ((), ())), preferred_element_type=jnp.float32)


def dot_nn(a, b):
    return jnp.dot(a, b, preferred_element_type=jnp.float32)


def kernel(
    mask, rows, width, sharp_ref, proj_ref, pos_ref, loss_ref, grad_ref,
    raw, q, inv, kb, st, wt, peak, total, spos, lse_own, ex, ex_in, rl, lse_rows, lse_keys,
    g_out, g_in, rad, rad_out, rad_in,
    own_sem, y_send, y_recv, k_send, k_recv, l_send, l_recv, e_send, e_recv, g_send, g_recv, r_send, r_recv,
):
    half = rows // 2
    step_rows = half // CHUNKS
    t = lax.axis_index("tour")
    f = lax.axis_index("feat")
    other = 1 - f
    peer = (t, other)
    near = {bit: (flipped(t, bit), f) for bit in (1, 2, 4)}
    far = [flipped(t, mask ^ j) for j in range(GROUP)]
    scale = sharp_ref[0, 0] * LOG2E

    barrier = pltpu.get_barrier_semaphore()
    everyone = [peer] + list(near.values()) + [(d, s) for d in far for s in (f, other)]
    for device in everyone:
        pl.semaphore_signal(barrier, inc=1, device_id=device, device_id_type=MESH)
    pl.semaphore_wait(barrier, len(everyone))

    def remote(src, dst, send, recv, device):
        return pltpu.make_async_remote_copy(
            src_ref=src, dst_ref=dst, send_sem=send, recv_sem=recv,
            device_id=device, device_id_type=MESH,
        )

    pieces = 4
    piece = half // pieces

    def y_copy(i):
        side = other if i < pieces else f
        spot = pl.ds(pl.multiple_of(side * half + (i % pieces) * piece, piece), piece)
        return remote(proj_ref.at[spot], raw.at[f, spot], y_send.at[i], y_recv.at[i], peer)

    for i in range(pieces):
        y_copy(i).start()
    own_copy = pltpu.make_async_copy(proj_ref, raw.at[f], own_sem)
    own_copy.start()
    own_copy.wait()

    def normalise(start, count):
        spot = pl.ds(start, count)
        left = raw[0, spot, :].astype(jnp.float32)
        right = raw[1, spot, :].astype(jnp.float32)
        squares = jnp.sum(left * left, -1, keepdims=True) + jnp.sum(right * right, -1, keepdims=True)
        inverse = lax.rsqrt(squares + EPSILON)
        q[0, spot, :] = (left * inverse).astype(jnp.bfloat16)
        q[1, spot, :] = (right * inverse).astype(jnp.bfloat16)
        inv[spot, :] = jnp.broadcast_to(inverse, (count, 128))

    send_rows = half // STEPS
    merged = STEPS // CHUNKS

    def landing(slot, n):
        spot = pl.ds(pl.multiple_of((n % merged) * send_rows, send_rows), send_rows)
        return kb.at[:, n // merged, slot, spot]

    def cross(n):
        spot = pl.ds(pl.multiple_of(f * half + n * send_rows, send_rows), send_rows)
        return remote(q.at[:, spot], landing(0, n), k_send.at[0, n], k_recv.at[0, n], (far[0], f))

    def forward(src, dst, bit, n):
        return remote(
            landing(src, n), landing(dst, n), k_send.at[dst, n], k_recv.at[dst, n], near[bit]
        )

    hops = {1: (0, 1), 2: (0, 2), 3: (2, 1), 4: (0, 4), 5: (4, 1), 6: (4, 2), 7: (6, 1)}

    def send_key(slot, n):
        if slot == 0:
            return cross(n)
        src, bit = hops[slot]
        return forward(src, slot, bit, n)

    for i in range(pieces):
        y_copy(i).wait_recv()
        normalise(pl.multiple_of(f * half + i * piece, piece), piece)
        for n in range(i * STEPS // pieces, (i + 1) * STEPS // pieces):
            if n < WINDOW:
                cross(n).start()
        y_copy(pieces + i).start()

    tile = 128

    def score(c, keys, own):
        for part in range(rows // 256):
            lanes = slice(part * 256, part * 256 + 256)
            block = (dot_nt(keys(0), q[0, lanes, :]) + dot_nt(keys(1), q[1, lanes, :])) * scale
            if own:
                key_ids = lax.broadcasted_iota(jnp.int32, block.shape, 0) + f * half
                query_ids = lax.broadcasted_iota(jnp.int32, block.shape, 1) + part * 256
                block = jnp.where(key_ids == query_ids, FAR, block)
                hit = key_ids == pos_ref[:, lanes]
                spos[:, lanes] = jnp.sum(jnp.where(hit, block, 0.0), 0, keepdims=True)
            for i in range(256 // tile):
                st[part * (256 // tile) + i, c] = block[:, i * tile : (i + 1) * tile]
            folded = block.reshape(half // 8, 8, 256)
            top = jnp.max(folded, 0)
            if own:
                peak[:, lanes] = top
                total[:, lanes] = jnp.sum(jnp.exp2(folded - top[None]), 0)
            else:
                old = peak[:, lanes]
                top = jnp.maximum(top, old)
                peak[:, lanes] = top
                total[:, lanes] = total[:, lanes] * jnp.exp2(old - top) + jnp.sum(
                    jnp.exp2(folded - top[None]), 0
                )

    def own_keys(h):
        return q[h, pl.ds(pl.multiple_of(f * half, half), half), :]

    def chunk_keys(c):
        return lambda h: kb[h, c].reshape(half, width)

    def tick(n):
        one, two, three = (n - lag for lag in LAGS)

        @pl.when(n < STEPS)
        def _():
            send_key(0, n).wait_recv()

            @pl.when(n + WINDOW < STEPS)
            def _():
                cross(n + WINDOW).start()

            for slot in (4, 2, 1):
                send_key(slot, n).start()

        @pl.when((one >= 0) & (one < STEPS))
        def _():
            send_key(4, one).wait_recv()
            send_key(6, one).start()
            send_key(5, one).start()
            send_key(2, one).wait_recv()
            send_key(3, one).start()

        @pl.when((two >= 0) & (two < STEPS))
        def _():
            send_key(6, two).wait_recv()
            send_key(7, two).start()

        @pl.when(three >= 0)
        def _():
            for slot in (1, 3, 5, 7):
                send_key(slot, three).wait_recv()

            @pl.when(three % merged == merged - 1)
            def _():
                score(three // merged, chunk_keys(three // merged), False)

    def tick_body(n, carry):
        tick(n)
        return carry

    lax.fori_loop(0, 3, tick_body, 0)
    for i in range(pieces):
        y_copy(pieces + i).wait_recv()
        normalise(pl.multiple_of(other * half + i * piece, piece), piece)
    score(CHUNKS, own_keys, True)
    lax.fori_loop(3, STEPS + LAGS[2], tick_body, 0)

    top = jnp.max(peak[...], 0, keepdims=True)
    share = jnp.sum(total[...] * jnp.exp2(peak[...] - top), 0, keepdims=True)
    mine = top + LOG2E * jnp.log(share)
    for h in range(2):
        ex[h] = mine[:, h * half : (h + 1) * half]
        ex[2 + h] = spos[:, h * half : (h + 1) * half]

    def lse_copy(j, h):
        side = f if h == 0 else other
        return remote(ex.at[side], rl.at[j, f], l_send.at[j, h], l_recv.at[j, f], (far[j], side))

    def lse_arrival(j, side):
        return remote(ex.at[0], rl.at[j, side], l_send.at[j, 0], l_recv.at[j, side], peer)

    ex_copy = remote(ex, ex_in, e_send, e_recv, peer)
    for j in range(GROUP - 1, -1, -1):
        for h in range(2):
            lse_copy(j, h).start()
    ex_copy.start()

    ex_copy.wait_recv()
    for h in range(2):
        lanes = slice(h * half, (h + 1) * half)
        lse_own[:, lanes] = log2_add(ex[h], ex_in[h])
        loss_ref[:, lanes] = LN2 * (lse_own[:, lanes] - (ex[2 + h] + ex_in[2 + h]))
    lse_rows[...] = jnp.zeros_like(lse_rows)
    lse_rows[pl.ds(GROUP, 1), :] = log2_add(ex[f], ex_in[f])
    for j in range(GROUP):
        for side in range(2):
            lse_arrival(j, side).wait_recv()
        lse_rows[pl.ds(j, 1), :] = log2_add(rl[j, 0], rl[j, 1])
    columns = lse_rows[...].T
    for j in range(GROUP):
        spread = jnp.broadcast_to(columns[:, j : j + 1], (half, 128))
        lse_keys[pl.ds(0, CHUNKS), j] = spread.reshape(CHUNKS, step_rows, 128)
    lse_keys[CHUNKS] = jnp.broadcast_to(columns[:, GROUP : GROUP + 1], (half, 128)).reshape(
        GROUP, step_rows, 128
    )

    tiles = rows // tile

    def keys_of(c, h):
        if c == CHUNKS:
            return own_keys(h)
        return kb[h, c].reshape(half, width)

    def g_copy(i):
        return remote(g_out.at[i], g_in.at[i], g_send.at[i], g_recv.at[i], peer)

    def send_tile(i, carry):
        lanes = pl.ds(pl.multiple_of(i * tile, tile), tile)
        lse_query = lse_own[:, lanes]
        acc = jnp.zeros((tile, width), jnp.float32)
        inner = jnp.zeros((8, tile), jnp.float32)
        for c in range(CHUNKS + 1):
            block = st[i, c]
            weight = jnp.exp2(block - lse_query) + jnp.exp2(block - lse_keys[c].reshape(half, 128))
            if c == CHUNKS:
                key_ids = lax.broadcasted_iota(jnp.int32, block.shape, 0) + f * half
                weight = weight - jnp.where(key_ids == pos_ref[:, lanes], 2.0, 0.0)
            rounded = weight.astype(jnp.bfloat16)
            turned = rounded.T
            wt[i, c] = turned
            inner = inner + jnp.sum(
                (rounded.astype(jnp.float32) * block).reshape(half // 8, 8, tile), 0
            )
            acc = acc + dot_nn(turned, keys_of(c, other))
        rad[:, lanes] = jnp.sum(inner, 0, keepdims=True)
        g_out[i] = acc.astype(jnp.bfloat16)
        g_copy(i).start()
        return carry

    lax.fori_loop(0, tiles, send_tile, 0)
    rad_out[0] = rad[...]
    rad_copy = remote(rad_out, rad_in, r_send, r_recv, peer)
    rad_copy.start()

    def keep_tile(i, carry):
        acc = jnp.zeros((tile, width), jnp.float32)
        for c in range(CHUNKS + 1):
            acc = acc + dot_nn(wt[i, c], keys_of(c, f))
        grad_ref[pl.ds(pl.multiple_of(i * tile, tile), tile), :] = acc
        return carry

    lax.fori_loop(0, tiles, keep_tile, 0)
    rad_copy.wait_recv()
    radial = jnp.broadcast_to(LN2 * (rad_out[0] + rad_in[0]), (128, rows)).T
    sharpness = sharp_ref[0, 0]
    for i in range(tiles):
        spot = slice(i * tile, (i + 1) * tile)
        g_copy(i).wait_recv()
        inverse = inv[spot, :1]
        unit = raw[f, spot, :].astype(jnp.float32) * inverse
        whole = (grad_ref[spot, :] + g_in[i].astype(jnp.float32)) * sharpness
        grad_ref[spot, :] = inverse * (whole - unit * radial[spot, :1])

    for i in range(2 * pieces):
        y_copy(i).wait_send()
    for slot in range(GROUP):
        for n in range(STEPS):
            send_key(slot, n).wait_send()
    for j in range(GROUP):
        for h in range(2):
            lse_copy(j, h).wait_send()
    ex_copy.wait_send()
    rad_copy.wait_send()
    for i in range(tiles):
        g_copy(i).wait_send()


def per_device(projected, sharpness, partners, positives):
    rows, width = projected.shape
    blocks = lax.axis_size("tour")
    if blocks != 2 * GROUP or lax.axis_size("feat") != 2:
        return per_device_any(projected, sharpness, partners, positives)
    half = rows // 2
    step_rows = half // CHUNKS
    tiles = rows // 128
    local_pos = (positives - lax.axis_index("tour") * rows)[None, :]
    bf16, f32 = jnp.bfloat16, jnp.float32
    dma = pltpu.SemaphoreType.DMA
    loss, grad = pl.pallas_call(
        functools.partial(kernel, GROUP, rows, width),
        out_shape=(
            jax.ShapeDtypeStruct((1, rows), f32),
            jax.ShapeDtypeStruct((rows, width), f32),
        ),
        in_specs=[
            pl.BlockSpec(memory_space=pltpu.SMEM),
            pl.BlockSpec(memory_space=pltpu.HBM),
            pl.BlockSpec(memory_space=pltpu.VMEM),
        ],
        out_specs=[pl.BlockSpec(memory_space=pltpu.VMEM)] * 2,
        scratch_shapes=[
            pltpu.VMEM((2, rows, width), bf16),
            pltpu.VMEM((2, rows, width), bf16),
            pltpu.VMEM((rows, 128), f32),
            pltpu.VMEM((2, CHUNKS, GROUP, step_rows, width), bf16),
            pltpu.VMEM((tiles, CHUNKS + 1, half, 128), f32),
            pltpu.VMEM((tiles, CHUNKS + 1, 128, half), bf16),
            pltpu.VMEM((8, rows), f32),
            pltpu.VMEM((8, rows), f32),
            pltpu.VMEM((1, rows), f32),
            pltpu.VMEM((1, rows), f32),
            pltpu.VMEM((4, 1, half), f32),
            pltpu.VMEM((4, 1, half), f32),
            pltpu.VMEM((GROUP, 2, 1, half), f32),
            pltpu.VMEM((128, half), f32),
            pltpu.VMEM((CHUNKS + 1, GROUP, step_rows, 128), f32),
            pltpu.VMEM((tiles, 128, width), bf16),
            pltpu.VMEM((tiles, 128, width), bf16),
            pltpu.VMEM((1, rows), f32),
            pltpu.VMEM((1, 1, rows), f32),
            pltpu.VMEM((1, 1, rows), f32),
            dma, dma((8,)), dma((8,)),
            dma((GROUP, STEPS)), dma((GROUP, STEPS)),
            dma((GROUP, 2)), dma((GROUP, 2)),
            dma, dma,
            dma((tiles,)), dma((tiles,)),
            dma, dma,
        ],
        compiler_params=pltpu.CompilerParams(
            collective_id=0, has_side_effects=True, vmem_limit_bytes=63 * 1024 * 1024
        ),
        cost_estimate=pl.CostEstimate(
            flops=9 * 4 * rows * half * 2 * width, bytes_accessed=4 * rows * width,
            transcendentals=27 * rows * half,
        ),
    )(sharpness.reshape(1, 1), projected, local_pos)
    return loss[0], grad


def solution(mesh):
    in_specs = (P("tour", "feat"), P(), P(), P("tour"))
    out_specs = (P("tour"), P("tour", "feat"))
    return jax.shard_map(
        per_device, mesh=mesh, in_specs=in_specs, out_specs=out_specs, check_vma=False
    )
```

```python
import functools
import math
from functools import reduce

import jax
import jax.numpy as jnp
from jax import lax
from jax.experimental import pallas as pl
from jax.experimental.pallas import tpu as pltpu
from jax.sharding import PartitionSpec as P

EPSILON = 1e-06


def from_partner(value, axis, stride):
    mask = 2**stride
    pairs = [(source, source ^ mask) for source in range(lax.axis_size(axis))]
    return lax.ppermute(value, axis, pairs)


def mask_bit(round_masks, bit_index):
    return jnp.bitwise_and(jnp.right_shift(round_masks, bit_index), 1) == 1


def deliver_each(block, round_masks, bits_count):
    routed = []
    for round_index in range(round_masks.shape[0]):
        moving = block
        for bit_index in range(bits_count):
            arrived = from_partner(moving, "tour", bit_index)
            moving = jnp.where(mask_bit(round_masks[round_index], bit_index), arrived, moving)
        routed.append(moving)
    return routed


def similar(queries, key_block):
    return jnp.einsum("qd,kd->qk", queries, key_block, preferred_element_type=jnp.float32)


def per_device_any(projected, sharpness, partners, positives):
    bits_count = lax.axis_size("tour").bit_length() - 1
    block_index = lax.axis_index("tour")
    row_count = projected.shape[0]
    round_masks = jnp.bitwise_xor(
        lax.dynamic_index_in_dim(partners, block_index, 1, keepdims=False), block_index
    )
    round_count = round_masks.shape[0]
    low_bits = round_count.bit_length() - 1
    high_mask = jnp.left_shift(jnp.right_shift(round_masks[0], low_bits), low_bits)
    code_masks = jnp.bitwise_xor(high_mask, jnp.arange(round_count, dtype=jnp.int32))
    local_pos = positives - block_index * row_count
    floats = projected.astype(jnp.float32)
    inverse = lax.rsqrt(lax.psum(jnp.sum(floats * floats, -1), "feat") + EPSILON)
    unit_rows = floats * inverse[:, None]
    embedded = unit_rows.astype(jnp.bfloat16)
    partner_blocks = deliver_each(embedded, code_masks, bits_count)

    def scored(key_block):
        return lax.psum(similar(embedded, key_block), "feat") * sharpness

    columns = jnp.arange(row_count, dtype=jnp.int32)[None, :]
    query_ids = jnp.arange(embedded.shape[0], dtype=jnp.int32)[:, None]
    own_scores = jnp.where(columns == query_ids, -jnp.inf, scored(embedded))
    all_scores = [own_scores] + [scored(key_block) for key_block in partner_blocks]
    row_peak = reduce(jnp.maximum, [jnp.max(block_scores, -1) for block_scores in all_scores])
    exp_total = reduce(
        jnp.add,
        [jnp.sum(jnp.exp(block_scores - row_peak[:, None]), -1) for block_scores in all_scores],
    )
    lse_rows = row_peak + jnp.log(exp_total)
    pos_hit = columns == local_pos[:, None]
    loss_rows = lse_rows - jnp.sum(jnp.where(pos_hit, own_scores, 0.0), -1)
    stacked = jnp.broadcast_to(lse_rows[None, :], (round_count, row_count))
    for bit_index in range(bits_count):
        arrived = from_partner(stacked, "tour", bit_index)
        stacked = jnp.where(mask_bit(code_masks, bit_index)[:, None], arrived, stacked)
    own_weight = (
        jnp.exp(own_scores - lse_rows[:, None])
        + jnp.exp(own_scores - lse_rows[None, :])
        - 2.0 * pos_hit.astype(jnp.float32)
    )
    unit_grad = jnp.dot(
        own_weight.astype(jnp.bfloat16), embedded, preferred_element_type=jnp.float32
    )
    for round_index in range(len(partner_blocks)):
        block_scores = all_scores[round_index + 1]
        weight = jnp.exp(block_scores - lse_rows[:, None]) + jnp.exp(
            block_scores - stacked[round_index][None, :]
        )
        unit_grad = unit_grad + jnp.dot(
            weight.astype(jnp.bfloat16),
            partner_blocks[round_index],
            preferred_element_type=jnp.float32,
        )
    unit_grad = unit_grad * sharpness
    radial = lax.psum(jnp.sum(unit_rows * unit_grad, -1), "feat")
    view_grad = inverse[:, None] * (unit_grad - unit_rows * radial[:, None])
    return (loss_rows, view_grad)


MESH = pl.DeviceIdType.MESH
LOG2E = math.log2(math.e)
LN2 = math.log(2.0)
GROUP = 8
CHUNKS = 8
STEPS = 16
WINDOW = 4
LAGS = (2, 4, 5)
FAR = -1e30


def flipped(index, mask):
    bit = 1
    while bit <= mask:
        if mask & bit:
            index = index + bit * (1 - 2 * ((index // bit) % 2))
        bit *= 2
    return index


def log2_add(a, b):
    return jnp.maximum(a, b) + LOG2E * jnp.log(1.0 + jnp.exp2(-jnp.abs(a - b)))


def dot(a, b):
    return jnp.dot(a, b, preferred_element_type=jnp.float32)


def kernel(
    mask, rows, width, sharp_ref, proj_ref, pos_ref, loss_ref, grad_ref,
    raw, q, turned, inv, keys, st, wt, peak, total, spos, lse_own, ex, ex_in, rl, lse_rows, lse_keys,
    g_out, g_in, rad, rad_out, rad_in,
    own_sem, y_send, y_recv, k_send, k_recv, l_send, l_recv, e_send, e_recv, g_send, g_recv, r_send, r_recv,
):
    half = rows // 2
    step_rows = half // CHUNKS
    t = lax.axis_index("tour")
    f = lax.axis_index("feat")
    other = 1 - f
    peer = (t, other)
    near = {bit: (flipped(t, bit), f) for bit in (1, 2, 4)}
    far = [flipped(t, mask ^ j) for j in range(GROUP)]
    scale = sharp_ref[0, 0] * LOG2E

    barrier = pltpu.get_barrier_semaphore()
    everyone = [peer] + list(near.values()) + [(d, s) for d in far for s in (f, other)]
    for device in everyone:
        pl.semaphore_signal(barrier, inc=1, device_id=device, device_id_type=MESH)
    pl.semaphore_wait(barrier, len(everyone))

    def remote(src, dst, send, recv, device):
        return pltpu.make_async_remote_copy(
            src_ref=src, dst_ref=dst, send_sem=send, recv_sem=recv,
            device_id=device, device_id_type=MESH,
        )

    pieces = 4
    piece = half // pieces

    def y_copy(i):
        side = other if i < pieces else f
        spot = pl.ds(pl.multiple_of(side * half + (i % pieces) * piece, piece), piece)
        return remote(proj_ref.at[spot], raw.at[f, spot], y_send.at[i], y_recv.at[i], peer)

    for i in range(pieces):
        y_copy(i).start()
    own_copy = pltpu.make_async_copy(proj_ref, raw.at[f], own_sem)
    own_copy.start()
    own_copy.wait()

    def normalise(start, count):
        spot = pl.ds(start, count)
        left = raw[0, spot, :].astype(jnp.float32)
        right = raw[1, spot, :].astype(jnp.float32)
        squares = jnp.sum(left * left, -1, keepdims=True) + jnp.sum(right * right, -1, keepdims=True)
        inverse = lax.rsqrt(squares + EPSILON)
        q[spot, :width] = (left * inverse).astype(jnp.bfloat16)
        q[spot, width:] = (right * inverse).astype(jnp.bfloat16)
        inv[spot, :] = jnp.broadcast_to(inverse, (count, 128))

    send_rows = half // STEPS
    merged = STEPS // CHUNKS

    def landing(slot, n):
        start = (n // merged) * half + slot * step_rows + (n % merged) * send_rows
        return keys.at[pl.ds(pl.multiple_of(start, send_rows), send_rows)]

    def cross(n):
        spot = pl.ds(pl.multiple_of(f * half + n * send_rows, send_rows), send_rows)
        return remote(q.at[spot], landing(0, n), k_send.at[0, n], k_recv.at[0, n], (far[0], f))

    def forward(src, dst, bit, n):
        return remote(
            landing(src, n), landing(dst, n), k_send.at[dst, n], k_recv.at[dst, n], near[bit]
        )

    hops = {1: (0, 1), 2: (0, 2), 3: (2, 1), 4: (0, 4), 5: (4, 1), 6: (4, 2), 7: (6, 1)}

    def send_key(slot, n):
        if slot == 0:
            return cross(n)
        src, bit = hops[slot]
        return forward(src, slot, bit, n)

    for i in range(pieces):
        y_copy(i).wait_recv()
        normalise(pl.multiple_of(f * half + i * piece, piece), piece)
        for n in range(i * STEPS // pieces, (i + 1) * STEPS // pieces):
            if n < WINDOW:
                cross(n).start()
        y_copy(pieces + i).start()

    tile = 128

    def score(c, own):
        for part in range(rows // 256):
            lanes = slice(part * 256, part * 256 + 256)
            chunk = keys[pl.ds(pl.multiple_of(c * half, half), half), :]
            block = dot(chunk, turned[:, lanes]) * scale
            if own:
                key_ids = lax.broadcasted_iota(jnp.int32, block.shape, 0) + f * half
                query_ids = lax.broadcasted_iota(jnp.int32, block.shape, 1) + part * 256
                block = jnp.where(key_ids == query_ids, FAR, block)
                hit = key_ids == pos_ref[:, lanes]
                spos[:, lanes] = jnp.sum(jnp.where(hit, block, 0.0), 0, keepdims=True)
            for i in range(256 // tile):
                st[part * (256 // tile) + i, c] = block[:, i * tile : (i + 1) * tile]
            folded = block.reshape(half // 8, 8, 256)
            top = jnp.max(folded, 0)
            if own:
                peak[:, lanes] = top
                total[:, lanes] = jnp.sum(jnp.exp2(folded - top[None]), 0)
            else:
                old = peak[:, lanes]
                top = jnp.maximum(top, old)
                peak[:, lanes] = top
                total[:, lanes] = total[:, lanes] * jnp.exp2(old - top) + jnp.sum(
                    jnp.exp2(folded - top[None]), 0
                )

    def tick(n):
        one, two, three = (n - lag for lag in LAGS)

        @pl.when(n < STEPS)
        def _():
            send_key(0, n).wait_recv()

            @pl.when(n + WINDOW < STEPS)
            def _():
                cross(n + WINDOW).start()

            for slot in (4, 2, 1):
                send_key(slot, n).start()

        @pl.when((one >= 0) & (one < STEPS))
        def _():
            send_key(4, one).wait_recv()
            send_key(6, one).start()
            send_key(5, one).start()
            send_key(2, one).wait_recv()
            send_key(3, one).start()

        @pl.when((two >= 0) & (two < STEPS))
        def _():
            send_key(6, two).wait_recv()
            send_key(7, two).start()

        @pl.when(three >= 0)
        def _():
            for slot in (1, 3, 5, 7):
                send_key(slot, three).wait_recv()

            @pl.when(three % merged == merged - 1)
            def _():
                score(three // merged, False)

    def tick_body(n, carry):
        tick(n)
        return carry

    lax.fori_loop(0, 3, tick_body, 0)
    for i in range(pieces):
        y_copy(pieces + i).wait_recv()
        normalise(pl.multiple_of(other * half + i * piece, piece), piece)
    turned[...] = q[...].T
    keys[pl.ds(CHUNKS * half, half), :] = q[pl.ds(pl.multiple_of(f * half, half), half), :]
    score(CHUNKS, True)
    lax.fori_loop(3, STEPS + LAGS[2], tick_body, 0)

    top = jnp.max(peak[...], 0, keepdims=True)
    share = jnp.sum(total[...] * jnp.exp2(peak[...] - top), 0, keepdims=True)
    mine = top + LOG2E * jnp.log(share)
    for h in range(2):
        ex[h] = mine[:, h * half : (h + 1) * half]
        ex[2 + h] = spos[:, h * half : (h + 1) * half]

    def lse_copy(j, h):
        side = f if h == 0 else other
        return remote(ex.at[side], rl.at[j, f], l_send.at[j, h], l_recv.at[j, f], (far[j], side))

    def lse_arrival(j, side):
        return remote(ex.at[0], rl.at[j, side], l_send.at[j, 0], l_recv.at[j, side], peer)

    ex_copy = remote(ex, ex_in, e_send, e_recv, peer)
    for j in range(GROUP - 1, -1, -1):
        for h in range(2):
            lse_copy(j, h).start()
    ex_copy.start()

    ex_copy.wait_recv()
    for h in range(2):
        lanes = slice(h * half, (h + 1) * half)
        lse_own[:, lanes] = log2_add(ex[h], ex_in[h])
        loss_ref[:, lanes] = LN2 * (lse_own[:, lanes] - (ex[2 + h] + ex_in[2 + h]))
    lse_rows[...] = jnp.zeros_like(lse_rows)
    lse_rows[pl.ds(GROUP, 1), :] = log2_add(ex[f], ex_in[f])
    for j in range(GROUP):
        for side in range(2):
            lse_arrival(j, side).wait_recv()
        lse_rows[pl.ds(j, 1), :] = log2_add(rl[j, 0], rl[j, 1])
    columns = lse_rows[...].T
    for j in range(GROUP):
        spread = jnp.broadcast_to(columns[:, j : j + 1], (half, 128))
        lse_keys[pl.ds(0, CHUNKS), j] = spread.reshape(CHUNKS, step_rows, 128)
    lse_keys[CHUNKS] = jnp.broadcast_to(columns[:, GROUP : GROUP + 1], (half, 128)).reshape(
        GROUP, step_rows, 128
    )

    tiles = rows // tile

    def side_keys(side):
        return keys[:, pl.ds(pl.multiple_of(side * width, width), width)]

    def g_copy(i):
        return remote(g_out.at[i], g_in.at[i], g_send.at[i], g_recv.at[i], peer)

    def send_tile(i, carry):
        lanes = pl.ds(pl.multiple_of(i * tile, tile), tile)
        lse_query = lse_own[:, lanes]
        inner = jnp.zeros((8, tile), jnp.float32)
        for c in range(CHUNKS + 1):
            block = st[i, c]
            weight = jnp.exp2(block - lse_query) + jnp.exp2(block - lse_keys[c].reshape(half, 128))
            if c == CHUNKS:
                key_ids = lax.broadcasted_iota(jnp.int32, block.shape, 0) + f * half
                weight = weight - jnp.where(key_ids == pos_ref[:, lanes], 2.0, 0.0)
            rounded = weight.astype(jnp.bfloat16)
            wt[i, :, c * half : (c + 1) * half] = rounded.T
            inner = inner + jnp.sum(
                (rounded.astype(jnp.float32) * block).reshape(half // 8, 8, tile), 0
            )
        rad[:, lanes] = jnp.sum(inner, 0, keepdims=True)
        g_out[i] = dot(wt[i], side_keys(other)).astype(jnp.bfloat16)
        g_copy(i).start()
        return carry

    lax.fori_loop(0, tiles, send_tile, 0)
    rad_out[0] = rad[...]
    rad_copy = remote(rad_out, rad_in, r_send, r_recv, peer)
    rad_copy.start()

    def keep_tiles(i, carry):
        weights = wt[pl.ds(2 * i, 2)].reshape(2 * tile, wt.shape[-1])
        spot = pl.ds(pl.multiple_of(i * 2 * tile, 2 * tile), 2 * tile)
        grad_ref[spot, :] = dot(weights, side_keys(f))
        return carry

    lax.fori_loop(0, tiles // 2, keep_tiles, 0)
    rad_copy.wait_recv()
    radial = jnp.broadcast_to(LN2 * (rad_out[0] + rad_in[0]), (128, rows)).T
    sharpness = sharp_ref[0, 0]
    for i in range(tiles):
        spot = slice(i * tile, (i + 1) * tile)
        g_copy(i).wait_recv()
        inverse = inv[spot, :1]
        unit = raw[f, spot, :].astype(jnp.float32) * inverse
        whole = (grad_ref[spot, :] + g_in[i].astype(jnp.float32)) * sharpness
        grad_ref[spot, :] = inverse * (whole - unit * radial[spot, :1])

    for i in range(2 * pieces):
        y_copy(i).wait_send()
    for slot in range(GROUP):
        for n in range(STEPS):
            send_key(slot, n).wait_send()
    for j in range(GROUP):
        for h in range(2):
            lse_copy(j, h).wait_send()
    ex_copy.wait_send()
    rad_copy.wait_send()
    for i in range(tiles):
        g_copy(i).wait_send()


def per_device(projected, sharpness, partners, positives):
    rows, width = projected.shape
    blocks = lax.axis_size("tour")
    if blocks != 2 * GROUP or lax.axis_size("feat") != 2:
        return per_device_any(projected, sharpness, partners, positives)
    half = rows // 2
    step_rows = half // CHUNKS
    tiles = rows // 128
    local_pos = (positives - lax.axis_index("tour") * rows)[None, :]
    bf16, f32 = jnp.bfloat16, jnp.float32
    dma = pltpu.SemaphoreType.DMA
    loss, grad = pl.pallas_call(
        functools.partial(kernel, GROUP, rows, width),
        out_shape=(
            jax.ShapeDtypeStruct((1, rows), f32),
            jax.ShapeDtypeStruct((rows, width), f32),
        ),
        in_specs=[
            pl.BlockSpec(memory_space=pltpu.SMEM),
            pl.BlockSpec(memory_space=pl.ANY),
            pl.BlockSpec(memory_space=pltpu.VMEM),
        ],
        out_specs=[pl.BlockSpec(memory_space=pltpu.VMEM)] * 2,
        scratch_shapes=[
            pltpu.VMEM((2, rows, width), bf16),
            pltpu.VMEM((rows, 2 * width), bf16),
            pltpu.VMEM((2 * width, rows), bf16),
            pltpu.VMEM((rows, 128), f32),
            pltpu.VMEM(((CHUNKS + 1) * half, 2 * width), bf16),
            pltpu.VMEM((tiles, CHUNKS + 1, half, 128), f32),
            pltpu.VMEM((tiles, 128, (CHUNKS + 1) * half), bf16),
            pltpu.VMEM((8, rows), f32),
            pltpu.VMEM((8, rows), f32),
            pltpu.VMEM((1, rows), f32),
            pltpu.VMEM((1, rows), f32),
            pltpu.VMEM((4, 1, half), f32),
            pltpu.VMEM((4, 1, half), f32),
            pltpu.VMEM((GROUP, 2, 1, half), f32),
            pltpu.VMEM((128, half), f32),
            pltpu.VMEM((CHUNKS + 1, GROUP, step_rows, 128), f32),
            pltpu.VMEM((tiles, 128, width), bf16),
            pltpu.VMEM((tiles, 128, width), bf16),
            pltpu.VMEM((1, rows), f32),
            pltpu.VMEM((1, 1, rows), f32),
            pltpu.VMEM((1, 1, rows), f32),
            dma, dma((8,)), dma((8,)),
            dma((GROUP, STEPS)), dma((GROUP, STEPS)),
            dma((GROUP, 2)), dma((GROUP, 2)),
            dma, dma,
            dma((tiles,)), dma((tiles,)),
            dma, dma,
        ],
        compiler_params=pltpu.CompilerParams(
            collective_id=0, has_side_effects=True, vmem_limit_bytes=50 * 1024 * 1024
        ),
        cost_estimate=pl.CostEstimate(
            flops=9 * 4 * rows * half * 2 * width, bytes_accessed=4 * rows * width,
            transcendentals=27 * rows * half,
        ),
    )(sharpness.reshape(1, 1), projected, local_pos)
    return loss[0], grad


def solution(mesh):
    in_specs = (P("tour", "feat"), P(), P(), P("tour"))
    out_specs = (P("tour"), P("tour", "feat"))
    return jax.shard_map(
        per_device, mesh=mesh, in_specs=in_specs, out_specs=out_specs, check_vma=False
    )
```

```python
import functools
import math
from functools import reduce

import jax
import jax.numpy as jnp
from jax import lax
from jax.experimental import pallas as pl
from jax.experimental.pallas import tpu as pltpu
from jax.sharding import PartitionSpec as P

EPSILON = 1e-06


def from_partner(value, axis, stride):
    mask = 2**stride
    pairs = [(source, source ^ mask) for source in range(lax.axis_size(axis))]
    return lax.ppermute(value, axis, pairs)


def mask_bit(round_masks, bit_index):
    return jnp.bitwise_and(jnp.right_shift(round_masks, bit_index), 1) == 1


def deliver_each(block, round_masks, bits_count):
    routed = []
    for round_index in range(round_masks.shape[0]):
        moving = block
        for bit_index in range(bits_count):
            arrived = from_partner(moving, "tour", bit_index)
            moving = jnp.where(mask_bit(round_masks[round_index], bit_index), arrived, moving)
        routed.append(moving)
    return routed


def similar(queries, key_block):
    return jnp.einsum("qd,kd->qk", queries, key_block, preferred_element_type=jnp.float32)


def per_device_any(projected, sharpness, partners, positives):
    bits_count = lax.axis_size("tour").bit_length() - 1
    block_index = lax.axis_index("tour")
    row_count = projected.shape[0]
    round_masks = jnp.bitwise_xor(
        lax.dynamic_index_in_dim(partners, block_index, 1, keepdims=False), block_index
    )
    round_count = round_masks.shape[0]
    low_bits = round_count.bit_length() - 1
    high_mask = jnp.left_shift(jnp.right_shift(round_masks[0], low_bits), low_bits)
    code_masks = jnp.bitwise_xor(high_mask, jnp.arange(round_count, dtype=jnp.int32))
    local_pos = positives - block_index * row_count
    floats = projected.astype(jnp.float32)
    inverse = lax.rsqrt(lax.psum(jnp.sum(floats * floats, -1), "feat") + EPSILON)
    unit_rows = floats * inverse[:, None]
    embedded = unit_rows.astype(jnp.bfloat16)
    partner_blocks = deliver_each(embedded, code_masks, bits_count)

    def scored(key_block):
        return lax.psum(similar(embedded, key_block), "feat") * sharpness

    columns = jnp.arange(row_count, dtype=jnp.int32)[None, :]
    query_ids = jnp.arange(embedded.shape[0], dtype=jnp.int32)[:, None]
    own_scores = jnp.where(columns == query_ids, -jnp.inf, scored(embedded))
    all_scores = [own_scores] + [scored(key_block) for key_block in partner_blocks]
    row_peak = reduce(jnp.maximum, [jnp.max(block_scores, -1) for block_scores in all_scores])
    exp_total = reduce(
        jnp.add,
        [jnp.sum(jnp.exp(block_scores - row_peak[:, None]), -1) for block_scores in all_scores],
    )
    lse_rows = row_peak + jnp.log(exp_total)
    pos_hit = columns == local_pos[:, None]
    loss_rows = lse_rows - jnp.sum(jnp.where(pos_hit, own_scores, 0.0), -1)
    stacked = jnp.broadcast_to(lse_rows[None, :], (round_count, row_count))
    for bit_index in range(bits_count):
        arrived = from_partner(stacked, "tour", bit_index)
        stacked = jnp.where(mask_bit(code_masks, bit_index)[:, None], arrived, stacked)
    own_weight = (
        jnp.exp(own_scores - lse_rows[:, None])
        + jnp.exp(own_scores - lse_rows[None, :])
        - 2.0 * pos_hit.astype(jnp.float32)
    )
    unit_grad = jnp.dot(
        own_weight.astype(jnp.bfloat16), embedded, preferred_element_type=jnp.float32
    )
    for round_index in range(len(partner_blocks)):
        block_scores = all_scores[round_index + 1]
        weight = jnp.exp(block_scores - lse_rows[:, None]) + jnp.exp(
            block_scores - stacked[round_index][None, :]
        )
        unit_grad = unit_grad + jnp.dot(
            weight.astype(jnp.bfloat16),
            partner_blocks[round_index],
            preferred_element_type=jnp.float32,
        )
    unit_grad = unit_grad * sharpness
    radial = lax.psum(jnp.sum(unit_rows * unit_grad, -1), "feat")
    view_grad = inverse[:, None] * (unit_grad - unit_rows * radial[:, None])
    return (loss_rows, view_grad)


MESH = pl.DeviceIdType.MESH
LOG2E = math.log2(math.e)
LN2 = math.log(2.0)
GROUP = 8
CHUNKS = 8
STEPS = 16
WINDOW = 6
LAGS = (3, 5, 8)
FAR = -1e30


def flipped(index, mask):
    bit = 1
    while bit <= mask:
        if mask & bit:
            index = index + bit * (1 - 2 * ((index // bit) % 2))
        bit *= 2
    return index


def log2_add(a, b):
    return jnp.maximum(a, b) + LOG2E * jnp.log(1.0 + jnp.exp2(-jnp.abs(a - b)))


def dot(a, b):
    return jnp.dot(a, b, preferred_element_type=jnp.float32)


def kernel(
    mask, rows, width, sharp_ref, proj_ref, pos_ref, loss_ref, grad_ref,
    raw, q, turned, inv, keys, st, wt, peak, total, spos, lse_own, ex, ex_in, rl, lse_rows, lse_keys,
    g_out, g_in, rad, rad_out, rad_in,
    own_sem, y_send, y_recv, k_send, k_recv, l_send, l_recv, e_send, e_recv, g_send, g_recv, r_send, r_recv,
):
    half = rows // 2
    step_rows = half // CHUNKS
    t = lax.axis_index("tour")
    f = lax.axis_index("feat")
    other = 1 - f
    peer = (t, other)
    near = {bit: (flipped(t, bit), f) for bit in (1, 2, 4)}
    far = [flipped(t, mask ^ j) for j in range(GROUP)]
    scale = sharp_ref[0, 0] * LOG2E

    barrier = pltpu.get_barrier_semaphore()
    everyone = [peer] + list(near.values()) + [(d, s) for d in far for s in (f, other)]
    for device in everyone:
        pl.semaphore_signal(barrier, inc=1, device_id=device, device_id_type=MESH)
    pl.semaphore_wait(barrier, len(everyone))

    def remote(src, dst, send, recv, device):
        return pltpu.make_async_remote_copy(
            src_ref=src, dst_ref=dst, send_sem=send, recv_sem=recv,
            device_id=device, device_id_type=MESH,
        )

    pieces = 4
    piece = half // pieces

    def y_copy(i):
        side = other if i < pieces else f
        spot = pl.ds(pl.multiple_of(side * half + (i % pieces) * piece, piece), piece)
        return remote(proj_ref.at[spot], raw.at[f, spot], y_send.at[i], y_recv.at[i], peer)

    for i in range(pieces):
        y_copy(i).start()
    own_copy = pltpu.make_async_copy(proj_ref, raw.at[f], own_sem)
    own_copy.start()
    own_copy.wait()

    def normalise(start, count):
        spot = pl.ds(start, count)
        left = raw[0, spot, :].astype(jnp.float32)
        right = raw[1, spot, :].astype(jnp.float32)
        squares = jnp.sum(left * left, -1, keepdims=True) + jnp.sum(right * right, -1, keepdims=True)
        inverse = lax.rsqrt(squares + EPSILON)
        q[spot, :width] = (left * inverse).astype(jnp.bfloat16)
        q[spot, width:] = (right * inverse).astype(jnp.bfloat16)
        inv[spot, :] = jnp.broadcast_to(inverse, (count, 128))

    send_rows = half // STEPS
    merged = STEPS // CHUNKS

    def landing(slot, n):
        start = (n // merged) * half + slot * step_rows + (n % merged) * send_rows
        return keys.at[pl.ds(pl.multiple_of(start, send_rows), send_rows)]

    def cross(n):
        spot = pl.ds(pl.multiple_of(f * half + n * send_rows, send_rows), send_rows)
        return remote(q.at[spot], landing(0, n), k_send.at[0, n], k_recv.at[0, n], (far[0], f))

    def forward(src, dst, bit, n):
        return remote(
            landing(src, n), landing(dst, n), k_send.at[dst, n], k_recv.at[dst, n], near[bit]
        )

    hops = {1: (0, 1), 2: (0, 2), 3: (2, 1), 4: (0, 4), 5: (4, 1), 6: (4, 2), 7: (6, 1)}

    def send_key(slot, n):
        if slot == 0:
            return cross(n)
        src, bit = hops[slot]
        return forward(src, slot, bit, n)

    for i in range(pieces):
        y_copy(i).wait_recv()
        normalise(pl.multiple_of(f * half + i * piece, piece), piece)
        for n in range(i * STEPS // pieces, (i + 1) * STEPS // pieces):
            if n < WINDOW:
                cross(n).start()
        y_copy(pieces + i).start()

    tile = 128

    def score(c, own):
        for part in range(rows // 256):
            lanes = slice(part * 256, part * 256 + 256)
            chunk = keys[pl.ds(pl.multiple_of(c * half, half), half), :]
            block = dot(chunk, turned[:, lanes]) * scale
            if own:
                key_ids = lax.broadcasted_iota(jnp.int32, block.shape, 0) + f * half
                query_ids = lax.broadcasted_iota(jnp.int32, block.shape, 1) + part * 256
                block = jnp.where(key_ids == query_ids, FAR, block)
                hit = key_ids == pos_ref[:, lanes]
                spos[:, lanes] = jnp.sum(jnp.where(hit, block, 0.0), 0, keepdims=True)
            for i in range(256 // tile):
                st[part * (256 // tile) + i, c] = block[:, i * tile : (i + 1) * tile]
            folded = block.reshape(half // 8, 8, 256)
            top = jnp.max(folded, 0)
            if own:
                peak[:, lanes] = top
                total[:, lanes] = jnp.sum(jnp.exp2(folded - top[None]), 0)
            else:
                old = peak[:, lanes]
                top = jnp.maximum(top, old)
                peak[:, lanes] = top
                total[:, lanes] = total[:, lanes] * jnp.exp2(old - top) + jnp.sum(
                    jnp.exp2(folded - top[None]), 0
                )

    def tick(n):
        one, two, three = (n - lag for lag in LAGS)

        @pl.when(n < STEPS)
        def _():
            send_key(0, n).wait_recv()

            @pl.when(n + WINDOW < STEPS)
            def _():
                cross(n + WINDOW).start()

            for slot in (4, 2, 1):
                send_key(slot, n).start()

        @pl.when((one >= 0) & (one < STEPS))
        def _():
            send_key(4, one).wait_recv()

            @pl.when(one % 2 == 0)
            def _():
                forward(4, 6, 2, one).start()

            send_key(5, one).start()
            send_key(2, one).wait_recv()

            @pl.when(one % 2 == 1)
            def _():
                forward(2, 6, 4, one).start()

            send_key(3, one).start()

        @pl.when((two >= 0) & (two < STEPS))
        def _():
            send_key(6, two).wait_recv()
            send_key(7, two).start()

        @pl.when(three >= 0)
        def _():
            for slot in (1, 3, 5, 7):
                send_key(slot, three).wait_recv()

            @pl.when(three % merged == merged - 1)
            def _():
                score(three // merged, False)

    def tick_body(n, carry):
        tick(n)
        return carry

    lax.fori_loop(0, 3, tick_body, 0)
    for i in range(pieces):
        y_copy(pieces + i).wait_recv()
        normalise(pl.multiple_of(other * half + i * piece, piece), piece)
    turned[...] = q[...].T
    keys[pl.ds(CHUNKS * half, half), :] = q[pl.ds(pl.multiple_of(f * half, half), half), :]
    score(CHUNKS, True)
    lax.fori_loop(3, STEPS + LAGS[2], tick_body, 0)

    top = jnp.max(peak[...], 0, keepdims=True)
    share = jnp.sum(total[...] * jnp.exp2(peak[...] - top), 0, keepdims=True)
    mine = top + LOG2E * jnp.log(share)
    for h in range(2):
        ex[h] = mine[:, h * half : (h + 1) * half]
        ex[2 + h] = spos[:, h * half : (h + 1) * half]

    def lse_copy(j, h):
        side = f if h == 0 else other
        return remote(ex.at[side], rl.at[j, f], l_send.at[j, h], l_recv.at[j, f], (far[j], side))

    def lse_arrival(j, side):
        return remote(ex.at[0], rl.at[j, side], l_send.at[j, 0], l_recv.at[j, side], peer)

    ex_copy = remote(ex, ex_in, e_send, e_recv, peer)
    for j in range(GROUP - 1, -1, -1):
        for h in range(2):
            lse_copy(j, h).start()
    ex_copy.start()

    ex_copy.wait_recv()
    for h in range(2):
        lanes = slice(h * half, (h + 1) * half)
        lse_own[:, lanes] = log2_add(ex[h], ex_in[h])
        loss_ref[:, lanes] = LN2 * (lse_own[:, lanes] - (ex[2 + h] + ex_in[2 + h]))
    lse_rows[...] = jnp.zeros_like(lse_rows)
    lse_rows[pl.ds(GROUP, 1), :] = log2_add(ex[f], ex_in[f])
    for j in range(GROUP):
        for side in range(2):
            lse_arrival(j, side).wait_recv()
        lse_rows[pl.ds(j, 1), :] = log2_add(rl[j, 0], rl[j, 1])
    columns = lse_rows[...].T
    for j in range(GROUP):
        spread = jnp.broadcast_to(columns[:, j : j + 1], (half, 128))
        lse_keys[pl.ds(0, CHUNKS), j] = spread.reshape(CHUNKS, step_rows, 128)
    lse_keys[CHUNKS] = jnp.broadcast_to(columns[:, GROUP : GROUP + 1], (half, 128)).reshape(
        GROUP, step_rows, 128
    )

    tiles = rows // tile

    def side_keys(side):
        return keys[:, pl.ds(pl.multiple_of(side * width, width), width)]

    def g_copy(i):
        return remote(g_out.at[i], g_in.at[i], g_send.at[i], g_recv.at[i], peer)

    def send_tile(i, carry):
        lanes = pl.ds(pl.multiple_of(i * tile, tile), tile)
        lse_query = lse_own[:, lanes]
        inner = jnp.zeros((8, tile), jnp.float32)
        for c in range(CHUNKS + 1):
            block = st[i, c]
            weight = jnp.exp2(block - lse_query) + jnp.exp2(block - lse_keys[c].reshape(half, 128))
            if c == CHUNKS:
                key_ids = lax.broadcasted_iota(jnp.int32, block.shape, 0) + f * half
                weight = weight - jnp.where(key_ids == pos_ref[:, lanes], 2.0, 0.0)
            rounded = weight.astype(jnp.bfloat16)
            wt[i, :, c * half : (c + 1) * half] = rounded.T
            inner = inner + jnp.sum(
                (rounded.astype(jnp.float32) * block).reshape(half // 8, 8, tile), 0
            )
        rad[:, lanes] = jnp.sum(inner, 0, keepdims=True)
        g_out[i] = dot(wt[i], side_keys(other)).astype(jnp.bfloat16)
        g_copy(i).start()
        return carry

    lax.fori_loop(0, tiles, send_tile, 0)
    rad_out[0] = rad[...]
    rad_copy = remote(rad_out, rad_in, r_send, r_recv, peer)
    rad_copy.start()

    def keep_tiles(i, carry):
        weights = wt[pl.ds(2 * i, 2)].reshape(2 * tile, wt.shape[-1])
        spot = pl.ds(pl.multiple_of(i * 2 * tile, 2 * tile), 2 * tile)
        grad_ref[spot, :] = dot(weights, side_keys(f))
        return carry

    lax.fori_loop(0, tiles // 2, keep_tiles, 0)
    rad_copy.wait_recv()
    radial = jnp.broadcast_to(LN2 * (rad_out[0] + rad_in[0]), (128, rows)).T
    sharpness = sharp_ref[0, 0]
    for i in range(tiles):
        spot = slice(i * tile, (i + 1) * tile)
        g_copy(i).wait_recv()
        inverse = inv[spot, :1]
        unit = raw[f, spot, :].astype(jnp.float32) * inverse
        whole = (grad_ref[spot, :] + g_in[i].astype(jnp.float32)) * sharpness
        grad_ref[spot, :] = inverse * (whole - unit * radial[spot, :1])

    for i in range(2 * pieces):
        y_copy(i).wait_send()
    for slot in range(GROUP):
        for n in range(STEPS):
            send_key(slot, n).wait_send()
    for j in range(GROUP):
        for h in range(2):
            lse_copy(j, h).wait_send()
    ex_copy.wait_send()
    rad_copy.wait_send()
    for i in range(tiles):
        g_copy(i).wait_send()


def per_device(projected, sharpness, partners, positives):
    rows, width = projected.shape
    blocks = lax.axis_size("tour")
    if blocks != 2 * GROUP or lax.axis_size("feat") != 2:
        return per_device_any(projected, sharpness, partners, positives)
    half = rows // 2
    step_rows = half // CHUNKS
    tiles = rows // 128
    local_pos = (positives - lax.axis_index("tour") * rows)[None, :]
    bf16, f32 = jnp.bfloat16, jnp.float32
    dma = pltpu.SemaphoreType.DMA
    loss, grad = pl.pallas_call(
        functools.partial(kernel, GROUP + GROUP // 2, rows, width),
        out_shape=(
            jax.ShapeDtypeStruct((1, rows), f32),
            jax.ShapeDtypeStruct((rows, width), f32),
        ),
        in_specs=[
            pl.BlockSpec(memory_space=pltpu.SMEM),
            pl.BlockSpec(memory_space=pl.ANY),
            pl.BlockSpec(memory_space=pltpu.VMEM),
        ],
        out_specs=[pl.BlockSpec(memory_space=pltpu.VMEM)] * 2,
        scratch_shapes=[
            pltpu.VMEM((2, rows, width), bf16),
            pltpu.VMEM((rows, 2 * width), bf16),
            pltpu.VMEM((2 * width, rows), bf16),
            pltpu.VMEM((rows, 128), f32),
            pltpu.VMEM(((CHUNKS + 1) * half, 2 * width), bf16),
            pltpu.VMEM((tiles, CHUNKS + 1, half, 128), f32),
            pltpu.VMEM((tiles, 128, (CHUNKS + 1) * half), bf16),
            pltpu.VMEM((8, rows), f32),
            pltpu.VMEM((8, rows), f32),
            pltpu.VMEM((1, rows), f32),
            pltpu.VMEM((1, rows), f32),
            pltpu.VMEM((4, 1, half), f32),
            pltpu.VMEM((4, 1, half), f32),
            pltpu.VMEM((GROUP, 2, 1, half), f32),
            pltpu.VMEM((128, half), f32),
            pltpu.VMEM((CHUNKS + 1, GROUP, step_rows, 128), f32),
            pltpu.VMEM((tiles, 128, width), bf16),
            pltpu.VMEM((tiles, 128, width), bf16),
            pltpu.VMEM((1, rows), f32),
            pltpu.VMEM((1, 1, rows), f32),
            pltpu.VMEM((1, 1, rows), f32),
            dma, dma((8,)), dma((8,)),
            dma((GROUP, STEPS)), dma((GROUP, STEPS)),
            dma((GROUP, 2)), dma((GROUP, 2)),
            dma, dma,
            dma((tiles,)), dma((tiles,)),
            dma, dma,
        ],
        compiler_params=pltpu.CompilerParams(
            collective_id=0, has_side_effects=True, vmem_limit_bytes=50 * 1024 * 1024
        ),
        cost_estimate=pl.CostEstimate(
            flops=9 * 4 * rows * half * 2 * width, bytes_accessed=4 * rows * width,
            transcendentals=27 * rows * half,
        ),
    )(sharpness.reshape(1, 1), projected, local_pos)
    return loss[0], grad


def solution(mesh):
    in_specs = (P("tour", "feat"), P(), P(), P("tour"))
    out_specs = (P("tour"), P("tour", "feat"))
    return jax.shard_map(
        per_device, mesh=mesh, in_specs=in_specs, out_specs=out_specs, check_vma=False
    )
```

```python
import functools
from functools import reduce

import jax
import jax.numpy as jnp
from jax import lax
from jax.experimental import pallas as pl
from jax.experimental.pallas import tpu as pltpu
from jax.sharding import PartitionSpec as P

EPSILON = 1e-06


def from_partner(value, axis, stride):
    mask = 2**stride
    pairs = [(source, source ^ mask) for source in range(lax.axis_size(axis))]
    return lax.ppermute(value, axis, pairs)


def mask_bit(round_masks, bit_index):
    return jnp.bitwise_and(jnp.right_shift(round_masks, bit_index), 1) == 1


def deliver_each(block, round_masks, bits_count):
    routed = []
    for round_index in range(round_masks.shape[0]):
        moving = block
        for bit_index in range(bits_count):
            arrived = from_partner(moving, "tour", bit_index)
            moving = jnp.where(mask_bit(round_masks[round_index], bit_index), arrived, moving)
        routed.append(moving)
    return routed


def similar(queries, key_block):
    return jnp.einsum("qd,kd->qk", queries, key_block, preferred_element_type=jnp.float32)


def per_device_any(projected, sharpness, partners, positives):
    bits_count = lax.axis_size("tour").bit_length() - 1
    block_index = lax.axis_index("tour")
    row_count = projected.shape[0]
    round_masks = jnp.bitwise_xor(
        lax.dynamic_index_in_dim(partners, block_index, 1, keepdims=False), block_index
    )
    round_count = round_masks.shape[0]
    low_bits = round_count.bit_length() - 1
    high_mask = jnp.left_shift(jnp.right_shift(round_masks[0], low_bits), low_bits)
    code_masks = jnp.bitwise_xor(high_mask, jnp.arange(round_count, dtype=jnp.int32))
    local_pos = positives - block_index * row_count
    floats = projected.astype(jnp.float32)
    inverse = lax.rsqrt(lax.psum(jnp.sum(floats * floats, -1), "feat") + EPSILON)
    unit_rows = floats * inverse[:, None]
    embedded = unit_rows.astype(jnp.bfloat16)
    partner_blocks = deliver_each(embedded, code_masks, bits_count)

    def scored(key_block):
        return lax.psum(similar(embedded, key_block), "feat") * sharpness

    columns = jnp.arange(row_count, dtype=jnp.int32)[None, :]
    query_ids = jnp.arange(embedded.shape[0], dtype=jnp.int32)[:, None]
    own_scores = jnp.where(columns == query_ids, -jnp.inf, scored(embedded))
    all_scores = [own_scores] + [scored(key_block) for key_block in partner_blocks]
    row_peak = reduce(jnp.maximum, [jnp.max(block_scores, -1) for block_scores in all_scores])
    exp_total = reduce(
        jnp.add,
        [jnp.sum(jnp.exp(block_scores - row_peak[:, None]), -1) for block_scores in all_scores],
    )
    lse_rows = row_peak + jnp.log(exp_total)
    pos_hit = columns == local_pos[:, None]
    loss_rows = lse_rows - jnp.sum(jnp.where(pos_hit, own_scores, 0.0), -1)
    stacked = jnp.broadcast_to(lse_rows[None, :], (round_count, row_count))
    for bit_index in range(bits_count):
        arrived = from_partner(stacked, "tour", bit_index)
        stacked = jnp.where(mask_bit(code_masks, bit_index)[:, None], arrived, stacked)
    own_weight = (
        jnp.exp(own_scores - lse_rows[:, None])
        + jnp.exp(own_scores - lse_rows[None, :])
        - 2.0 * pos_hit.astype(jnp.float32)
    )
    unit_grad = jnp.dot(
        own_weight.astype(jnp.bfloat16), embedded, preferred_element_type=jnp.float32
    )
    for round_index in range(len(partner_blocks)):
        block_scores = all_scores[round_index + 1]
        weight = jnp.exp(block_scores - lse_rows[:, None]) + jnp.exp(
            block_scores - stacked[round_index][None, :]
        )
        unit_grad = unit_grad + jnp.dot(
            weight.astype(jnp.bfloat16),
            partner_blocks[round_index],
            preferred_element_type=jnp.float32,
        )
    unit_grad = unit_grad * sharpness
    radial = lax.psum(jnp.sum(unit_rows * unit_grad, -1), "feat")
    view_grad = inverse[:, None] * (unit_grad - unit_rows * radial[:, None])
    return (loss_rows, view_grad)


MESH = pl.DeviceIdType.MESH
GROUP = 8
CHUNKS = 8
STEPS = 16
WINDOW = 6
LAGS = (3, 5, 8)
FAR = -1e30


def flipped(index, mask):
    bit = 1
    while bit <= mask:
        if mask & bit:
            index = index + bit * (1 - 2 * ((index // bit) % 2))
        bit *= 2
    return index


def log_add(a, b):
    return jnp.maximum(a, b) + jnp.log(1.0 + jnp.exp(-jnp.abs(a - b)))


def dot(a, b):
    return jnp.dot(a, b, preferred_element_type=jnp.float32)


def kernel(
    mask, rows, width, sharp_ref, proj_ref, pos_ref, loss_ref, grad_ref,
    raw, q, turned, inv, keys, st, wt, peak, total, spos, lse_own, ex, ex_in, rl, lse_rows, lse_keys,
    g_out, g_in, rad, rad_out, rad_in,
    own_sem, y_send, y_recv, k_send, k_recv, l_send, l_recv, e_send, e_recv, g_send, g_recv, r_send, r_recv,
):
    half = rows // 2
    step_rows = half // CHUNKS
    t = lax.axis_index("tour")
    f = lax.axis_index("feat")
    other = 1 - f
    peer = (t, other)
    near = {bit: (flipped(t, bit), f) for bit in (1, 2, 4)}
    far = [flipped(t, mask ^ j) for j in range(GROUP)]
    scale = sharp_ref[0, 0]

    barrier = pltpu.get_barrier_semaphore()
    everyone = [peer] + list(near.values()) + [(d, s) for d in far for s in (f, other)]
    for device in everyone:
        pl.semaphore_signal(barrier, inc=1, device_id=device, device_id_type=MESH)
    pl.semaphore_wait(barrier, len(everyone))

    def remote(src, dst, send, recv, device):
        return pltpu.make_async_remote_copy(
            src_ref=src, dst_ref=dst, send_sem=send, recv_sem=recv,
            device_id=device, device_id_type=MESH,
        )

    pieces = 4
    piece = half // pieces

    def y_copy(i):
        side = other if i < pieces else f
        spot = pl.ds(pl.multiple_of(side * half + (i % pieces) * piece, piece), piece)
        return remote(proj_ref.at[spot], raw.at[f, spot], y_send.at[i], y_recv.at[i], peer)

    for i in range(pieces):
        y_copy(i).start()
    own_copy = pltpu.make_async_copy(proj_ref, raw.at[f], own_sem)
    own_copy.start()
    own_copy.wait()

    def normalise(start, count):
        spot = pl.ds(start, count)
        left = raw[0, spot, :].astype(jnp.float32)
        right = raw[1, spot, :].astype(jnp.float32)
        squares = jnp.sum(left * left, -1, keepdims=True) + jnp.sum(right * right, -1, keepdims=True)
        inverse = lax.rsqrt(squares + EPSILON)
        q[spot, :width] = (left * inverse).astype(jnp.bfloat16)
        q[spot, width:] = (right * inverse).astype(jnp.bfloat16)
        inv[spot, :] = jnp.broadcast_to(inverse, (count, 128))

    send_rows = half // STEPS
    merged = STEPS // CHUNKS

    def landing(slot, n):
        start = (n // merged) * half + slot * step_rows + (n % merged) * send_rows
        return keys.at[pl.ds(pl.multiple_of(start, send_rows), send_rows)]

    def cross(n, slot=0):
        spot = pl.ds(pl.multiple_of(f * half + n * send_rows, send_rows), send_rows)
        return remote(
            q.at[spot], landing(slot, n), k_send.at[slot, n], k_recv.at[slot, n], (far[slot], f)
        )

    def forward(src, dst, bit, n):
        return remote(
            landing(src, n), landing(dst, n), k_send.at[dst, n], k_recv.at[dst, n], near[bit]
        )

    hops = {2: (0, 2), 3: (2, 1), 4: (0, 4), 5: (4, 1), 6: (4, 2), 7: (6, 1)}

    def send_key(slot, n):
        if slot < 2:
            return cross(n, slot)
        src, bit = hops[slot]
        return forward(src, slot, bit, n)

    for i in range(pieces):
        y_copy(i).wait_recv()
        normalise(pl.multiple_of(f * half + i * piece, piece), piece)
        for n in range(i * STEPS // pieces, (i + 1) * STEPS // pieces):
            if n < WINDOW:
                cross(n).start()
                cross(n, 1).start()
        y_copy(pieces + i).start()

    tile = 128

    def score(c, own):
        for part in range(rows // 256):
            lanes = slice(part * 256, part * 256 + 256)
            chunk = keys[pl.ds(pl.multiple_of(c * half, half), half), :]
            block = dot(chunk, turned[:, lanes]) * scale
            if own:
                key_ids = lax.broadcasted_iota(jnp.int32, block.shape, 0) + f * half
                query_ids = lax.broadcasted_iota(jnp.int32, block.shape, 1) + part * 256
                block = jnp.where(key_ids == query_ids, FAR, block)
                hit = key_ids == pos_ref[:, lanes]
                spos[:, lanes] = jnp.sum(jnp.where(hit, block, 0.0), 0, keepdims=True)
            for i in range(256 // tile):
                st[part * (256 // tile) + i, c] = block[:, i * tile : (i + 1) * tile]
            folded = block.reshape(half // 8, 8, 256)
            top = jnp.max(folded, 0)
            if own:
                peak[:, lanes] = top
                total[:, lanes] = jnp.sum(jnp.exp(folded - top[None]), 0)
            else:
                old = peak[:, lanes]
                top = jnp.maximum(top, old)
                peak[:, lanes] = top
                total[:, lanes] = total[:, lanes] * jnp.exp(old - top) + jnp.sum(
                    jnp.exp(folded - top[None]), 0
                )

    def tick(n):
        one, two, three = (n - lag for lag in LAGS)

        @pl.when(n < STEPS)
        def _():
            send_key(0, n).wait_recv()

            @pl.when(n + WINDOW < STEPS)
            def _():
                cross(n + WINDOW).start()
                cross(n + WINDOW, 1).start()

            for slot in (4, 2):
                send_key(slot, n).start()
            send_key(1, n).wait_recv()

            @pl.when(n % 4 == 0)
            def _():
                forward(1, 5, 4, n).start()
                forward(1, 3, 2, n).start()

        @pl.when((one >= 0) & (one < STEPS))
        def _():
            send_key(4, one).wait_recv()

            @pl.when(one % 2 == 0)
            def _():
                forward(4, 6, 2, one).start()

            @pl.when(one % 4 > 0)
            def _():
                send_key(5, one).start()

            send_key(2, one).wait_recv()

            @pl.when(one % 2 == 1)
            def _():
                forward(2, 6, 4, one).start()

            @pl.when(one % 4 > 0)
            def _():
                send_key(3, one).start()

        @pl.when((two >= 0) & (two < STEPS))
        def _():
            send_key(6, two).wait_recv()
            send_key(7, two).start()

        @pl.when(three >= 0)
        def _():
            for slot in (3, 5, 7):
                send_key(slot, three).wait_recv()

            @pl.when(three % merged == merged - 1)
            def _():
                score(three // merged, False)

    def tick_body(n, carry):
        tick(n)
        return carry

    lax.fori_loop(0, 3, tick_body, 0)
    for i in range(pieces):
        y_copy(pieces + i).wait_recv()
        normalise(pl.multiple_of(other * half + i * piece, piece), piece)
    turned[...] = q[...].T
    keys[pl.ds(CHUNKS * half, half), :] = q[pl.ds(pl.multiple_of(f * half, half), half), :]
    score(CHUNKS, True)
    lax.fori_loop(3, STEPS + LAGS[2], tick_body, 0)

    top = jnp.max(peak[...], 0, keepdims=True)
    share = jnp.sum(total[...] * jnp.exp(peak[...] - top), 0, keepdims=True)
    mine = top + jnp.log(share)
    for h in range(2):
        ex[h] = mine[:, h * half : (h + 1) * half]
        ex[2 + h] = spos[:, h * half : (h + 1) * half]

    def lse_copy(j, h):
        side = f if h == 0 else other
        return remote(ex.at[side], rl.at[j, f], l_send.at[j, h], l_recv.at[j, f], (far[j], side))

    def lse_arrival(j, side):
        return remote(ex.at[0], rl.at[j, side], l_send.at[j, 0], l_recv.at[j, side], peer)

    ex_copy = remote(ex, ex_in, e_send, e_recv, peer)
    for j in range(GROUP - 1, -1, -1):
        for h in range(2):
            lse_copy(j, h).start()
    ex_copy.start()

    ex_copy.wait_recv()
    for h in range(2):
        lanes = slice(h * half, (h + 1) * half)
        lse_own[:, lanes] = log_add(ex[h], ex_in[h])
        loss_ref[:, lanes] = lse_own[:, lanes] - (ex[2 + h] + ex_in[2 + h])
    lse_rows[...] = jnp.zeros_like(lse_rows)
    lse_rows[pl.ds(GROUP, 1), :] = log_add(ex[f], ex_in[f])
    for j in range(GROUP):
        for side in range(2):
            lse_arrival(j, side).wait_recv()
        lse_rows[pl.ds(j, 1), :] = log_add(rl[j, 0], rl[j, 1])
    columns = lse_rows[...].T
    for j in range(GROUP):
        spread = jnp.broadcast_to(columns[:, j : j + 1], (half, 128))
        lse_keys[pl.ds(0, CHUNKS), j] = spread.reshape(CHUNKS, step_rows, 128)
    lse_keys[CHUNKS] = jnp.broadcast_to(columns[:, GROUP : GROUP + 1], (half, 128)).reshape(
        GROUP, step_rows, 128
    )

    tiles = rows // tile

    def side_keys(side):
        return keys[:, pl.ds(pl.multiple_of(side * width, width), width)]

    def g_copy(i):
        return remote(g_out.at[i], g_in.at[i], g_send.at[i], g_recv.at[i], peer)

    def send_tile(i, carry):
        lanes = pl.ds(pl.multiple_of(i * tile, tile), tile)
        lse_query = lse_own[:, lanes]
        inner = jnp.zeros((8, tile), jnp.float32)
        for c in range(CHUNKS + 1):
            block = st[i, c]
            weight = jnp.exp(block - lse_query) + jnp.exp(block - lse_keys[c].reshape(half, 128))
            if c == CHUNKS:
                key_ids = lax.broadcasted_iota(jnp.int32, block.shape, 0) + f * half
                weight = weight - jnp.where(key_ids == pos_ref[:, lanes], 2.0, 0.0)
            rounded = weight.astype(jnp.bfloat16)
            wt[i, :, c * half : (c + 1) * half] = rounded.T
            inner = inner + jnp.sum(
                (rounded.astype(jnp.float32) * block).reshape(half // 8, 8, tile), 0
            )
        rad[:, lanes] = jnp.sum(inner, 0, keepdims=True)
        g_out[i] = dot(wt[i], side_keys(other)).astype(jnp.bfloat16)
        g_copy(i).start()
        return carry

    lax.fori_loop(0, tiles, send_tile, 0)
    rad_out[0] = rad[...]
    rad_copy = remote(rad_out, rad_in, r_send, r_recv, peer)
    rad_copy.start()

    def keep_tiles(i, carry):
        weights = wt[pl.ds(2 * i, 2)].reshape(2 * tile, wt.shape[-1])
        spot = pl.ds(pl.multiple_of(i * 2 * tile, 2 * tile), 2 * tile)
        grad_ref[spot, :] = dot(weights, side_keys(f))
        return carry

    lax.fori_loop(0, tiles // 2, keep_tiles, 0)
    rad_copy.wait_recv()
    radial = jnp.broadcast_to(rad_out[0] + rad_in[0], (128, rows)).T
    sharpness = sharp_ref[0, 0]
    for i in range(tiles):
        spot = slice(i * tile, (i + 1) * tile)
        g_copy(i).wait_recv()
        inverse = inv[spot, :1]
        unit = raw[f, spot, :].astype(jnp.float32) * inverse
        whole = (grad_ref[spot, :] + g_in[i].astype(jnp.float32)) * sharpness
        grad_ref[spot, :] = inverse * (whole - unit * radial[spot, :1])

    for i in range(2 * pieces):
        y_copy(i).wait_send()
    for slot in range(GROUP):
        for n in range(STEPS):
            send_key(slot, n).wait_send()
    for j in range(GROUP):
        for h in range(2):
            lse_copy(j, h).wait_send()
    ex_copy.wait_send()
    rad_copy.wait_send()
    for i in range(tiles):
        g_copy(i).wait_send()


def per_device(projected, sharpness, partners, positives):
    rows, width = projected.shape
    blocks = lax.axis_size("tour")
    if blocks != 2 * GROUP or lax.axis_size("feat") != 2:
        return per_device_any(projected, sharpness, partners, positives)
    half = rows // 2
    step_rows = half // CHUNKS
    tiles = rows // 128
    local_pos = (positives - lax.axis_index("tour") * rows)[None, :]
    bf16, f32 = jnp.bfloat16, jnp.float32
    dma = pltpu.SemaphoreType.DMA
    loss, grad = pl.pallas_call(
        functools.partial(kernel, GROUP + GROUP // 2, rows, width),
        out_shape=(
            jax.ShapeDtypeStruct((1, rows), f32),
            jax.ShapeDtypeStruct((rows, width), f32),
        ),
        in_specs=[
            pl.BlockSpec(memory_space=pltpu.SMEM),
            pl.BlockSpec(memory_space=pl.ANY),
            pl.BlockSpec(memory_space=pltpu.VMEM),
        ],
        out_specs=[pl.BlockSpec(memory_space=pltpu.VMEM)] * 2,
        scratch_shapes=[
            pltpu.VMEM((2, rows, width), bf16),
            pltpu.VMEM((rows, 2 * width), bf16),
            pltpu.VMEM((2 * width, rows), bf16),
            pltpu.VMEM((rows, 128), f32),
            pltpu.VMEM(((CHUNKS + 1) * half, 2 * width), bf16),
            pltpu.VMEM((tiles, CHUNKS + 1, half, 128), f32),
            pltpu.VMEM((tiles, 128, (CHUNKS + 1) * half), bf16),
            pltpu.VMEM((8, rows), f32),
            pltpu.VMEM((8, rows), f32),
            pltpu.VMEM((1, rows), f32),
            pltpu.VMEM((1, rows), f32),
            pltpu.VMEM((4, 1, half), f32),
            pltpu.VMEM((4, 1, half), f32),
            pltpu.VMEM((GROUP, 2, 1, half), f32),
            pltpu.VMEM((128, half), f32),
            pltpu.VMEM((CHUNKS + 1, GROUP, step_rows, 128), f32),
            pltpu.VMEM((tiles, 128, width), bf16),
            pltpu.VMEM((tiles, 128, width), bf16),
            pltpu.VMEM((1, rows), f32),
            pltpu.VMEM((1, 1, rows), f32),
            pltpu.VMEM((1, 1, rows), f32),
            dma, dma((8,)), dma((8,)),
            dma((GROUP, STEPS)), dma((GROUP, STEPS)),
            dma((GROUP, 2)), dma((GROUP, 2)),
            dma, dma,
            dma((tiles,)), dma((tiles,)),
            dma, dma,
        ],
        compiler_params=pltpu.CompilerParams(
            collective_id=0, has_side_effects=True, vmem_limit_bytes=50 * 1024 * 1024
        ),
        cost_estimate=pl.CostEstimate(
            flops=9 * 4 * rows * half * 2 * width, bytes_accessed=4 * rows * width,
            transcendentals=27 * rows * half,
        ),
    )(sharpness.reshape(1, 1), projected, local_pos)
    return loss[0], grad


def solution(mesh):
    in_specs = (P("tour", "feat"), P(), P(), P("tour"))
    out_specs = (P("tour"), P("tour", "feat"))
    return jax.shard_map(
        per_device, mesh=mesh, in_specs=in_specs, out_specs=out_specs, check_vma=False
    )
```

```python
import functools
from functools import reduce

import jax
import jax.numpy as jnp
from jax import lax
from jax.experimental import pallas as pl
from jax.experimental.pallas import tpu as pltpu
from jax.sharding import PartitionSpec as P

EPSILON = 1e-06


def from_partner(value, axis, stride):
    mask = 2**stride
    pairs = [(source, source ^ mask) for source in range(lax.axis_size(axis))]
    return lax.ppermute(value, axis, pairs)


def mask_bit(round_masks, bit_index):
    return jnp.bitwise_and(jnp.right_shift(round_masks, bit_index), 1) == 1


def deliver_each(block, round_masks, bits_count):
    routed = []
    for round_index in range(round_masks.shape[0]):
        moving = block
        for bit_index in range(bits_count):
            arrived = from_partner(moving, "tour", bit_index)
            moving = jnp.where(mask_bit(round_masks[round_index], bit_index), arrived, moving)
        routed.append(moving)
    return routed


def similar(queries, key_block):
    return jnp.einsum("qd,kd->qk", queries, key_block, preferred_element_type=jnp.float32)


def per_device_any(projected, sharpness, partners, positives):
    bits_count = lax.axis_size("tour").bit_length() - 1
    block_index = lax.axis_index("tour")
    row_count = projected.shape[0]
    round_masks = jnp.bitwise_xor(
        lax.dynamic_index_in_dim(partners, block_index, 1, keepdims=False), block_index
    )
    round_count = round_masks.shape[0]
    low_bits = round_count.bit_length() - 1
    high_mask = jnp.left_shift(jnp.right_shift(round_masks[0], low_bits), low_bits)
    code_masks = jnp.bitwise_xor(high_mask, jnp.arange(round_count, dtype=jnp.int32))
    local_pos = positives - block_index * row_count
    floats = projected.astype(jnp.float32)
    inverse = lax.rsqrt(lax.psum(jnp.sum(floats * floats, -1), "feat") + EPSILON)
    unit_rows = floats * inverse[:, None]
    embedded = unit_rows.astype(jnp.bfloat16)
    partner_blocks = deliver_each(embedded, code_masks, bits_count)

    def scored(key_block):
        return lax.psum(similar(embedded, key_block), "feat") * sharpness

    columns = jnp.arange(row_count, dtype=jnp.int32)[None, :]
    query_ids = jnp.arange(embedded.shape[0], dtype=jnp.int32)[:, None]
    own_scores = jnp.where(columns == query_ids, -jnp.inf, scored(embedded))
    all_scores = [own_scores] + [scored(key_block) for key_block in partner_blocks]
    row_peak = reduce(jnp.maximum, [jnp.max(block_scores, -1) for block_scores in all_scores])
    exp_total = reduce(
        jnp.add,
        [jnp.sum(jnp.exp(block_scores - row_peak[:, None]), -1) for block_scores in all_scores],
    )
    lse_rows = row_peak + jnp.log(exp_total)
    pos_hit = columns == local_pos[:, None]
    loss_rows = lse_rows - jnp.sum(jnp.where(pos_hit, own_scores, 0.0), -1)
    stacked = jnp.broadcast_to(lse_rows[None, :], (round_count, row_count))
    for bit_index in range(bits_count):
        arrived = from_partner(stacked, "tour", bit_index)
        stacked = jnp.where(mask_bit(code_masks, bit_index)[:, None], arrived, stacked)
    own_weight = (
        jnp.exp(own_scores - lse_rows[:, None])
        + jnp.exp(own_scores - lse_rows[None, :])
        - 2.0 * pos_hit.astype(jnp.float32)
    )
    unit_grad = jnp.dot(
        own_weight.astype(jnp.bfloat16), embedded, preferred_element_type=jnp.float32
    )
    for round_index in range(len(partner_blocks)):
        block_scores = all_scores[round_index + 1]
        weight = jnp.exp(block_scores - lse_rows[:, None]) + jnp.exp(
            block_scores - stacked[round_index][None, :]
        )
        unit_grad = unit_grad + jnp.dot(
            weight.astype(jnp.bfloat16),
            partner_blocks[round_index],
            preferred_element_type=jnp.float32,
        )
    unit_grad = unit_grad * sharpness
    radial = lax.psum(jnp.sum(unit_rows * unit_grad, -1), "feat")
    view_grad = inverse[:, None] * (unit_grad - unit_rows * radial[:, None])
    return (loss_rows, view_grad)


MESH = pl.DeviceIdType.MESH
GROUP = 8
CHUNKS = 8
STEPS = 16
WINDOW = 6
LAGS = (2, 4, 6)
FAR = -1e30


def flipped(index, mask):
    bit = 1
    while bit <= mask:
        if mask & bit:
            index = index + bit * (1 - 2 * ((index // bit) % 2))
        bit *= 2
    return index


def log_add(a, b):
    return jnp.maximum(a, b) + jnp.log(1.0 + jnp.exp(-jnp.abs(a - b)))


def dot_nt(a, b):
    return lax.dot_general(a, b, (((1,), (1,)), ((), ())), preferred_element_type=jnp.float32)


def dot(a, b):
    return jnp.dot(a, b, preferred_element_type=jnp.float32)


def kernel(
    mask, rows, width, sharp_ref, proj_ref, pos_ref, loss_ref, grad_ref,
    raw, q, pos_col, lse_col, inv, keys, st, wt, peak, total, spos, lse_own, ex, ex_in, rl, lse_rows, lse_keys,
    g_out, g_in, rad, rad_out, rad_in,
    own_sem, y_send, y_recv, k_send, k_recv, l_send, l_recv, e_send, e_recv, g_send, g_recv, r_send, r_recv,
):
    half = rows // 2
    step_rows = half // CHUNKS
    t = lax.axis_index("tour")
    f = lax.axis_index("feat")
    other = 1 - f
    peer = (t, other)
    near = {bit: (flipped(t, bit), f) for bit in (1, 2, 4)}
    far = [flipped(t, mask ^ j) for j in range(GROUP)]
    scale = sharp_ref[0, 0]

    barrier = pltpu.get_barrier_semaphore()
    everyone = [peer] + list(near.values()) + [(d, s) for d in far for s in (f, other)]
    for device in everyone:
        pl.semaphore_signal(barrier, inc=1, device_id=device, device_id_type=MESH)
    pl.semaphore_wait(barrier, len(everyone))

    def remote(src, dst, send, recv, device):
        return pltpu.make_async_remote_copy(
            src_ref=src, dst_ref=dst, send_sem=send, recv_sem=recv,
            device_id=device, device_id_type=MESH,
        )

    pieces = 4
    piece = half // pieces

    def y_copy(i):
        side = other if i < pieces else f
        spot = pl.ds(pl.multiple_of(side * half + (i % pieces) * piece, piece), piece)
        return remote(proj_ref.at[spot], raw.at[f, spot], y_send.at[i], y_recv.at[i], peer)

    for i in range(pieces):
        y_copy(i).start()
    own_copy = pltpu.make_async_copy(proj_ref, raw.at[f], own_sem)
    own_copy.start()
    own_copy.wait()

    def normalise(start, count):
        spot = pl.ds(start, count)
        left = raw[0, spot, :].astype(jnp.float32)
        right = raw[1, spot, :].astype(jnp.float32)
        squares = jnp.sum(left * left, -1, keepdims=True) + jnp.sum(right * right, -1, keepdims=True)
        inverse = lax.rsqrt(squares + EPSILON)
        q[spot, :width] = (left * inverse).astype(jnp.bfloat16)
        q[spot, width:] = (right * inverse).astype(jnp.bfloat16)
        inv[spot, :] = jnp.broadcast_to(inverse, (count, 128))

    send_rows = half // STEPS
    merged = STEPS // CHUNKS

    def landing(slot, n):
        start = (n // merged) * half + slot * step_rows + (n % merged) * send_rows
        return keys.at[pl.ds(pl.multiple_of(start, send_rows), send_rows)]

    def cross(n):
        spot = pl.ds(pl.multiple_of(f * half + n * send_rows, send_rows), send_rows)
        return remote(q.at[spot], landing(0, n), k_send.at[0, n], k_recv.at[0, n], (far[0], f))

    def forward(src, dst, bit, n):
        return remote(
            landing(src, n), landing(dst, n), k_send.at[dst, n], k_recv.at[dst, n], near[bit]
        )

    hops = {1: (0, 1), 2: (0, 2), 3: (2, 1), 4: (0, 4), 5: (4, 1), 6: (4, 2), 7: (6, 1)}

    def send_key(slot, n):
        if slot == 0:
            return cross(n)
        src, bit = hops[slot]
        return forward(src, slot, bit, n)

    for i in range(pieces):
        y_copy(i).wait_recv()
        normalise(pl.multiple_of(f * half + i * piece, piece), piece)
        for n in range(i * STEPS // pieces, (i + 1) * STEPS // pieces):
            if n < WINDOW:
                cross(n).start()
        y_copy(pieces + i).start()

    tile = 128
    pos_col[...] = jnp.broadcast_to(pos_ref[...], (128, rows)).T

    def score(c, own):
        chunk = keys[pl.ds(pl.multiple_of(c * half, half), half), :]
        for part in range(rows // 256):
            spot = slice(part * 256, part * 256 + 256)
            block = dot_nt(q[spot, :], chunk) * scale
            if own:
                key_ids = lax.broadcasted_iota(jnp.int32, block.shape, 1) + f * half
                query_ids = lax.broadcasted_iota(jnp.int32, block.shape, 0) + part * 256
                block = jnp.where(key_ids == query_ids, FAR, block)
                hits = jnp.where(key_ids == pos_col[spot, :1], block, 0.0)
                spos[spot, :] = hits[:, :128] + hits[:, 128:]
            st[c, spot, :] = block
            left, right = block[:, :128], block[:, 128:]
            top = jnp.maximum(left, right)
            if own:
                peak[spot, :] = top
                total[spot, :] = jnp.exp(left - top) + jnp.exp(right - top)
            else:
                old = peak[spot, :]
                top = jnp.maximum(top, old)
                peak[spot, :] = top
                total[spot, :] = (
                    total[spot, :] * jnp.exp(old - top) + jnp.exp(left - top) + jnp.exp(right - top)
                )

    def tick(n):
        one, two, three = (n - lag for lag in LAGS)

        @pl.when(n < STEPS)
        def _():
            send_key(0, n).wait_recv()

            @pl.when(n + WINDOW < STEPS)
            def _():
                cross(n + WINDOW).start()

            for slot in (4, 2, 1):
                send_key(slot, n).start()

        @pl.when((one >= 0) & (one < STEPS))
        def _():
            send_key(4, one).wait_recv()
            send_key(6, one).start()
            send_key(5, one).start()
            send_key(2, one).wait_recv()
            send_key(3, one).start()

        @pl.when((two >= 0) & (two < STEPS))
        def _():
            send_key(6, two).wait_recv()
            send_key(7, two).start()

        @pl.when(three >= 0)
        def _():
            for slot in (1, 3, 5, 7):
                send_key(slot, three).wait_recv()

            @pl.when(three % merged == merged - 1)
            def _():
                score(three // merged, False)

    def tick_body(n, carry):
        tick(n)
        return carry

    lax.fori_loop(0, 3, tick_body, 0)
    for i in range(pieces):
        y_copy(pieces + i).wait_recv()
        normalise(pl.multiple_of(other * half + i * piece, piece), piece)
    keys[pl.ds(CHUNKS * half, half), :] = q[pl.ds(pl.multiple_of(f * half, half), half), :]
    score(CHUNKS, True)
    lax.fori_loop(3, STEPS + LAGS[2], tick_body, 0)

    peaks = peak[...].T
    top = jnp.max(peaks, 0, keepdims=True)
    share = jnp.sum(total[...].T * jnp.exp(peaks - top), 0, keepdims=True)
    mine = top + jnp.log(share)
    paired = jnp.sum(spos[...].T, 0, keepdims=True)
    for h in range(2):
        ex[h] = mine[:, h * half : (h + 1) * half]
        ex[2 + h] = paired[:, h * half : (h + 1) * half]

    def lse_copy(j, h):
        side = f if h == 0 else other
        return remote(ex.at[side], rl.at[j, f], l_send.at[j, h], l_recv.at[j, f], (far[j], side))

    def lse_arrival(j, side):
        return remote(ex.at[0], rl.at[j, side], l_send.at[j, 0], l_recv.at[j, side], peer)

    ex_copy = remote(ex, ex_in, e_send, e_recv, peer)
    for j in range(GROUP - 1, -1, -1):
        for h in range(2):
            lse_copy(j, h).start()
    ex_copy.start()

    ex_copy.wait_recv()
    for h in range(2):
        lanes = slice(h * half, (h + 1) * half)
        lse_own[:, lanes] = log_add(ex[h], ex_in[h])
        loss_ref[:, lanes] = lse_own[:, lanes] - (ex[2 + h] + ex_in[2 + h])
    lse_rows[...] = jnp.zeros_like(lse_rows)
    lse_rows[pl.ds(GROUP, 1), :] = log_add(ex[f], ex_in[f])
    for j in range(GROUP):
        for side in range(2):
            lse_arrival(j, side).wait_recv()
        lse_rows[pl.ds(j, 1), :] = log_add(rl[j, 0], rl[j, 1])
    lse_col[...] = jnp.broadcast_to(lse_own[...], (128, rows)).T
    columns = lse_rows[...].T
    lane_ids = lax.broadcasted_iota(jnp.int32, (step_rows, 128), 1)
    parts = []
    for j in range(GROUP):
        spread = jnp.broadcast_to(columns[:, j : j + 1], (half, 128))
        part = jnp.zeros((step_rows, 128), jnp.float32)
        for c in range(CHUNKS):
            part = jnp.where(lane_ids == c, spread[c * step_rows : (c + 1) * step_rows], part)
        parts.append(part)
    lse_keys[...] = jnp.concatenate(parts, 0).T

    tiles = rows // tile

    def side_keys(side):
        return keys[:, pl.ds(pl.multiple_of(side * width, width), width)]

    def g_copy(i):
        return remote(g_out.at[i], g_in.at[i], g_send.at[i], g_recv.at[i], peer)

    def send_tile(i, carry):
        spot = pl.ds(pl.multiple_of(i * tile, tile), tile)
        lse_query = lse_col[spot, :]
        inner = jnp.zeros((tile, 128), jnp.float32)
        for c in range(CHUNKS + 1):
            row = lse_keys[c : c + 1, :] if c < CHUNKS else lse_rows[GROUP : GROUP + 1, :]
            for h in range(half // 128):
                lanes = slice(h * 128, (h + 1) * 128)
                block = st[c, spot, lanes]
                weight = jnp.exp(block - lse_query) + jnp.exp(block - row[:, lanes])
                if c == CHUNKS:
                    key_ids = lax.broadcasted_iota(jnp.int32, block.shape, 1) + f * half + h * 128
                    weight = weight - jnp.where(key_ids == pos_col[spot, :], 2.0, 0.0)
                rounded = weight.astype(jnp.bfloat16)
                wt[spot, c * half + h * 128 : c * half + (h + 1) * 128] = rounded
                inner = inner + rounded.astype(jnp.float32) * block
        rad[spot, :] = inner
        g_out[i] = dot(wt[spot, :], side_keys(other)).astype(jnp.bfloat16)
        g_copy(i).start()
        return carry

    lax.fori_loop(0, tiles, send_tile, 0)
    rad_out[0] = jnp.sum(rad[...].T, 0, keepdims=True)
    rad_copy = remote(rad_out, rad_in, r_send, r_recv, peer)
    rad_copy.start()

    def keep_tiles(i, carry):
        spot = pl.ds(pl.multiple_of(i * 2 * tile, 2 * tile), 2 * tile)
        grad_ref[spot, :] = dot(wt[spot, :], side_keys(f))
        return carry

    lax.fori_loop(0, tiles // 2, keep_tiles, 0)
    rad_copy.wait_recv()
    radial = jnp.broadcast_to(rad_out[0] + rad_in[0], (128, rows)).T
    sharpness = sharp_ref[0, 0]
    for i in range(tiles):
        spot = slice(i * tile, (i + 1) * tile)
        g_copy(i).wait_recv()
        inverse = inv[spot, :1]
        unit = raw[f, spot, :].astype(jnp.float32) * inverse
        whole = (grad_ref[spot, :] + g_in[i].astype(jnp.float32)) * sharpness
        grad_ref[spot, :] = inverse * (whole - unit * radial[spot, :1])

    for i in range(2 * pieces):
        y_copy(i).wait_send()
    for slot in range(GROUP):
        for n in range(STEPS):
            send_key(slot, n).wait_send()
    for j in range(GROUP):
        for h in range(2):
            lse_copy(j, h).wait_send()
    ex_copy.wait_send()
    rad_copy.wait_send()
    for i in range(tiles):
        g_copy(i).wait_send()


def per_device(projected, sharpness, partners, positives):
    rows, width = projected.shape
    blocks = lax.axis_size("tour")
    if blocks != 2 * GROUP or lax.axis_size("feat") != 2:
        return per_device_any(projected, sharpness, partners, positives)
    half = rows // 2
    step_rows = half // CHUNKS
    tiles = rows // 128
    local_pos = (positives - lax.axis_index("tour") * rows)[None, :]
    bf16, f32 = jnp.bfloat16, jnp.float32
    dma = pltpu.SemaphoreType.DMA
    loss, grad = pl.pallas_call(
        functools.partial(kernel, GROUP, rows, width),
        out_shape=(
            jax.ShapeDtypeStruct((1, rows), f32),
            jax.ShapeDtypeStruct((rows, width), f32),
        ),
        in_specs=[
            pl.BlockSpec(memory_space=pltpu.SMEM),
            pl.BlockSpec(memory_space=pl.ANY),
            pl.BlockSpec(memory_space=pltpu.VMEM),
        ],
        out_specs=[pl.BlockSpec(memory_space=pltpu.VMEM)] * 2,
        scratch_shapes=[
            pltpu.VMEM((2, rows, width), bf16),
            pltpu.VMEM((rows, 2 * width), bf16),
            pltpu.VMEM((rows, 128), jnp.int32),
            pltpu.VMEM((rows, 128), f32),
            pltpu.VMEM((rows, 128), f32),
            pltpu.VMEM(((CHUNKS + 1) * half, 2 * width), bf16),
            pltpu.VMEM((CHUNKS + 1, rows, half), f32),
            pltpu.VMEM((rows, (CHUNKS + 1) * half), bf16),
            pltpu.VMEM((rows, 128), f32),
            pltpu.VMEM((rows, 128), f32),
            pltpu.VMEM((rows, 128), f32),
            pltpu.VMEM((1, rows), f32),
            pltpu.VMEM((4, 1, half), f32),
            pltpu.VMEM((4, 1, half), f32),
            pltpu.VMEM((GROUP, 2, 1, half), f32),
            pltpu.VMEM((128, half), f32),
            pltpu.VMEM((128, half), f32),
            pltpu.VMEM((tiles, 128, width), bf16),
            pltpu.VMEM((tiles, 128, width), bf16),
            pltpu.VMEM((rows, 128), f32),
            pltpu.VMEM((1, 1, rows), f32),
            pltpu.VMEM((1, 1, rows), f32),
            dma, dma((8,)), dma((8,)),
            dma((GROUP, STEPS)), dma((GROUP, STEPS)),
            dma((GROUP, 2)), dma((GROUP, 2)),
            dma, dma,
            dma((tiles,)), dma((tiles,)),
            dma, dma,
        ],
        compiler_params=pltpu.CompilerParams(
            collective_id=0, has_side_effects=True, vmem_limit_bytes=50 * 1024 * 1024
        ),
        cost_estimate=pl.CostEstimate(
            flops=9 * 4 * rows * half * 2 * width, bytes_accessed=4 * rows * width,
            transcendentals=27 * rows * half,
        ),
    )(sharpness.reshape(1, 1), projected, local_pos)
    return loss[0], grad


def solution(mesh):
    in_specs = (P("tour", "feat"), P(), P(), P("tour"))
    out_specs = (P("tour"), P("tour", "feat"))
    return jax.shard_map(
        per_device, mesh=mesh, in_specs=in_specs, out_specs=out_specs, check_vma=False
    )
```

```python
import functools
import math
from functools import reduce

import jax
import jax.numpy as jnp
from jax import lax
from jax.experimental import pallas as pl
from jax.experimental.pallas import tpu as pltpu
from jax.sharding import PartitionSpec as P

EPSILON = 1e-06


def from_partner(value, axis, stride):
    mask = 2**stride
    pairs = [(source, source ^ mask) for source in range(lax.axis_size(axis))]
    return lax.ppermute(value, axis, pairs)


def mask_bit(round_masks, bit_index):
    return jnp.bitwise_and(jnp.right_shift(round_masks, bit_index), 1) == 1


def deliver_each(block, round_masks, bits_count):
    routed = []
    for round_index in range(round_masks.shape[0]):
        moving = block
        for bit_index in range(bits_count):
            arrived = from_partner(moving, "tour", bit_index)
            moving = jnp.where(mask_bit(round_masks[round_index], bit_index), arrived, moving)
        routed.append(moving)
    return routed


def similar(queries, key_block):
    return jnp.einsum("qd,kd->qk", queries, key_block, preferred_element_type=jnp.float32)


def per_device_any(projected, sharpness, partners, positives):
    bits_count = lax.axis_size("tour").bit_length() - 1
    block_index = lax.axis_index("tour")
    row_count = projected.shape[0]
    round_masks = jnp.bitwise_xor(
        lax.dynamic_index_in_dim(partners, block_index, 1, keepdims=False), block_index
    )
    round_count = round_masks.shape[0]
    low_bits = round_count.bit_length() - 1
    high_mask = jnp.left_shift(jnp.right_shift(round_masks[0], low_bits), low_bits)
    code_masks = jnp.bitwise_xor(high_mask, jnp.arange(round_count, dtype=jnp.int32))
    local_pos = positives - block_index * row_count
    floats = projected.astype(jnp.float32)
    inverse = lax.rsqrt(lax.psum(jnp.sum(floats * floats, -1), "feat") + EPSILON)
    unit_rows = floats * inverse[:, None]
    embedded = unit_rows.astype(jnp.bfloat16)
    partner_blocks = deliver_each(embedded, code_masks, bits_count)

    def scored(key_block):
        return lax.psum(similar(embedded, key_block), "feat") * sharpness

    columns = jnp.arange(row_count, dtype=jnp.int32)[None, :]
    query_ids = jnp.arange(embedded.shape[0], dtype=jnp.int32)[:, None]
    own_scores = jnp.where(columns == query_ids, -jnp.inf, scored(embedded))
    all_scores = [own_scores] + [scored(key_block) for key_block in partner_blocks]
    row_peak = reduce(jnp.maximum, [jnp.max(block_scores, -1) for block_scores in all_scores])
    exp_total = reduce(
        jnp.add,
        [jnp.sum(jnp.exp(block_scores - row_peak[:, None]), -1) for block_scores in all_scores],
    )
    lse_rows = row_peak + jnp.log(exp_total)
    pos_hit = columns == local_pos[:, None]
    loss_rows = lse_rows - jnp.sum(jnp.where(pos_hit, own_scores, 0.0), -1)
    stacked = jnp.broadcast_to(lse_rows[None, :], (round_count, row_count))
    for bit_index in range(bits_count):
        arrived = from_partner(stacked, "tour", bit_index)
        stacked = jnp.where(mask_bit(code_masks, bit_index)[:, None], arrived, stacked)
    own_weight = (
        jnp.exp(own_scores - lse_rows[:, None])
        + jnp.exp(own_scores - lse_rows[None, :])
        - 2.0 * pos_hit.astype(jnp.float32)
    )
    unit_grad = jnp.dot(
        own_weight.astype(jnp.bfloat16), embedded, preferred_element_type=jnp.float32
    )
    for round_index in range(len(partner_blocks)):
        block_scores = all_scores[round_index + 1]
        weight = jnp.exp(block_scores - lse_rows[:, None]) + jnp.exp(
            block_scores - stacked[round_index][None, :]
        )
        unit_grad = unit_grad + jnp.dot(
            weight.astype(jnp.bfloat16),
            partner_blocks[round_index],
            preferred_element_type=jnp.float32,
        )
    unit_grad = unit_grad * sharpness
    radial = lax.psum(jnp.sum(unit_rows * unit_grad, -1), "feat")
    view_grad = inverse[:, None] * (unit_grad - unit_rows * radial[:, None])
    return (loss_rows, view_grad)


MESH = pl.DeviceIdType.MESH
LOG2E = math.log2(math.e)
LN2 = math.log(2.0)
GROUP = 8
CHUNKS = 8
STEPS = 16
WINDOW = 2
LAGS = (2, 4, 6)
FAR = -1e30


def flipped(index, mask):
    bit = 1
    while bit <= mask:
        if mask & bit:
            index = index + bit * (1 - 2 * ((index // bit) % 2))
        bit *= 2
    return index


def log2_add(a, b):
    return jnp.maximum(a, b) + LOG2E * jnp.log(1.0 + jnp.exp2(-jnp.abs(a - b)))


def dot(a, b):
    return jnp.dot(a, b, preferred_element_type=jnp.float32)


def kernel(
    mask, rows, width, sharp_ref, proj_ref, pos_ref, loss_ref, grad_ref,
    raw, q, turned, inv, keys, st, wt, peak, total, spos, lse_own, ex, ex_in, rl, lse_rows, lse_keys,
    g_out, g_in, rad, rad_out, rad_in,
    own_sem, y_send, y_recv, k_send, k_recv, l_send, l_recv, e_send, e_recv, g_send, g_recv, r_send, r_recv,
):
    half = rows // 2
    step_rows = half // CHUNKS
    t = lax.axis_index("tour")
    f = lax.axis_index("feat")
    other = 1 - f
    peer = (t, other)
    near = {bit: (flipped(t, bit), f) for bit in (1, 2, 4)}
    far = [flipped(t, mask ^ j) for j in range(GROUP)]
    scale = sharp_ref[0, 0] * LOG2E

    barrier = pltpu.get_barrier_semaphore()
    everyone = [peer] + list(near.values()) + [(d, s) for d in far for s in (f, other)]
    for device in everyone:
        pl.semaphore_signal(barrier, inc=1, device_id=device, device_id_type=MESH)
    pl.semaphore_wait(barrier, len(everyone))

    def remote(src, dst, send, recv, device):
        return pltpu.make_async_remote_copy(
            src_ref=src, dst_ref=dst, send_sem=send, recv_sem=recv,
            device_id=device, device_id_type=MESH,
        )

    pieces = 4
    piece = half // pieces

    def y_copy(i):
        side = other if i < pieces else f
        spot = pl.ds(pl.multiple_of(side * half + (i % pieces) * piece, piece), piece)
        return remote(proj_ref.at[spot], raw.at[f, spot], y_send.at[i], y_recv.at[i], peer)

    for i in range(pieces):
        y_copy(i).start()
    own_copy = pltpu.make_async_copy(proj_ref, raw.at[f], own_sem)
    own_copy.start()
    own_copy.wait()

    def normalise(start, count):
        spot = pl.ds(start, count)
        left = raw[0, spot, :].astype(jnp.float32)
        right = raw[1, spot, :].astype(jnp.float32)
        squares = jnp.sum(left * left, -1, keepdims=True) + jnp.sum(right * right, -1, keepdims=True)
        inverse = lax.rsqrt(squares + EPSILON)
        q[spot, :width] = (left * inverse).astype(jnp.bfloat16)
        q[spot, width:] = (right * inverse).astype(jnp.bfloat16)
        inv[spot, :] = jnp.broadcast_to(inverse, (count, 128))

    send_rows = half // STEPS
    merged = STEPS // CHUNKS

    def landing(slot, n):
        start = (n // merged) * half + slot * step_rows + (n % merged) * send_rows
        return keys.at[pl.ds(pl.multiple_of(start, send_rows), send_rows)]

    def cross(n):
        spot = pl.ds(pl.multiple_of(f * half + n * send_rows, send_rows), send_rows)
        return remote(q.at[spot], landing(0, n), k_send.at[0, n], k_recv.at[0, n], (far[0], f))

    def forward(src, dst, bit, n):
        return remote(
            landing(src, n), landing(dst, n), k_send.at[dst, n], k_recv.at[dst, n], near[bit]
        )

    hops = {1: (0, 1), 2: (0, 2), 3: (2, 1), 4: (0, 4), 5: (4, 1), 6: (4, 2), 7: (6, 1)}

    def send_key(slot, n):
        if slot == 0:
            return cross(n)
        src, bit = hops[slot]
        return forward(src, slot, bit, n)

    for i in range(pieces):
        y_copy(i).wait_recv()
        normalise(pl.multiple_of(f * half + i * piece, piece), piece)
        for n in range(i * STEPS // pieces, (i + 1) * STEPS // pieces):
            if n < WINDOW:
                cross(n).start()
        y_copy(pieces + i).start()

    tile = 128

    def score(c, own):
        for part in range(rows // 256):
            lanes = slice(part * 256, part * 256 + 256)
            chunk = keys[pl.ds(pl.multiple_of(c * half, half), half), :]
            block = dot(chunk, turned[:, lanes]) * scale
            if own:
                key_ids = lax.broadcasted_iota(jnp.int32, block.shape, 0) + f * half
                query_ids = lax.broadcasted_iota(jnp.int32, block.shape, 1) + part * 256
                block = jnp.where(key_ids == query_ids, FAR, block)
                hit = key_ids == pos_ref[:, lanes]
                spos[:, lanes] = jnp.sum(jnp.where(hit, block, 0.0), 0, keepdims=True)
            for i in range(256 // tile):
                st[part * (256 // tile) + i, c] = block[:, i * tile : (i + 1) * tile]
            folded = block.reshape(half // 8, 8, 256)
            top = jnp.max(folded, 0)
            if own:
                peak[:, lanes] = top
                total[:, lanes] = jnp.sum(jnp.exp2(folded - top[None]), 0)
            else:
                old = peak[:, lanes]
                top = jnp.maximum(top, old)
                peak[:, lanes] = top
                total[:, lanes] = total[:, lanes] * jnp.exp2(old - top) + jnp.sum(
                    jnp.exp2(folded - top[None]), 0
                )

    def tick(n):
        one, two, three = (n - lag for lag in LAGS)

        @pl.when(n < STEPS)
        def _():
            send_key(0, n).wait_recv()

            for slot in (4, 2, 1):
                send_key(slot, n).start()

            @pl.when(n + WINDOW < STEPS)
            def _():
                cross(n + WINDOW).start()

        @pl.when((one >= 0) & (one < STEPS))
        def _():
            send_key(4, one).wait_recv()
            send_key(6, one).start()
            send_key(5, one).start()
            send_key(2, one).wait_recv()
            send_key(3, one).start()

        @pl.when((two >= 0) & (two < STEPS))
        def _():
            send_key(6, two).wait_recv()
            send_key(7, two).start()

        @pl.when(three >= 0)
        def _():
            for slot in (1, 3, 5, 7):
                send_key(slot, three).wait_recv()

            @pl.when(three % merged == merged - 1)
            def _():
                score(three // merged, False)

    def tick_body(n, carry):
        tick(n)
        return carry

    lax.fori_loop(0, 3, tick_body, 0)
    for i in range(pieces):
        y_copy(pieces + i).wait_recv()
        normalise(pl.multiple_of(other * half + i * piece, piece), piece)
    turned[...] = q[...].T
    keys[pl.ds(CHUNKS * half, half), :] = q[pl.ds(pl.multiple_of(f * half, half), half), :]
    score(CHUNKS, True)
    lax.fori_loop(3, STEPS + LAGS[2], tick_body, 0)

    top = jnp.max(peak[...], 0, keepdims=True)
    share = jnp.sum(total[...] * jnp.exp2(peak[...] - top), 0, keepdims=True)
    mine = top + LOG2E * jnp.log(share)
    for h in range(2):
        ex[h] = mine[:, h * half : (h + 1) * half]
        ex[2 + h] = spos[:, h * half : (h + 1) * half]

    def lse_copy(j, h):
        side = f if h == 0 else other
        return remote(ex.at[side], rl.at[j, f], l_send.at[j, h], l_recv.at[j, f], (far[j], side))

    def lse_arrival(j, side):
        return remote(ex.at[0], rl.at[j, side], l_send.at[j, 0], l_recv.at[j, side], peer)

    ex_copy = remote(ex, ex_in, e_send, e_recv, peer)
    for j in range(GROUP - 1, -1, -1):
        for h in range(2):
            lse_copy(j, h).start()
    ex_copy.start()

    ex_copy.wait_recv()
    for h in range(2):
        lanes = slice(h * half, (h + 1) * half)
        lse_own[:, lanes] = log2_add(ex[h], ex_in[h])
        loss_ref[:, lanes] = LN2 * (lse_own[:, lanes] - (ex[2 + h] + ex_in[2 + h]))
    lse_rows[...] = jnp.zeros_like(lse_rows)
    lse_rows[pl.ds(GROUP, 1), :] = log2_add(ex[f], ex_in[f])
    for j in range(GROUP):
        for side in range(2):
            lse_arrival(j, side).wait_recv()
        lse_rows[pl.ds(j, 1), :] = log2_add(rl[j, 0], rl[j, 1])
    columns = lse_rows[...].T
    for j in range(GROUP):
        spread = jnp.broadcast_to(columns[:, j : j + 1], (half, 128))
        lse_keys[pl.ds(0, CHUNKS), j] = spread.reshape(CHUNKS, step_rows, 128)
    lse_keys[CHUNKS] = jnp.broadcast_to(columns[:, GROUP : GROUP + 1], (half, 128)).reshape(
        GROUP, step_rows, 128
    )

    tiles = rows // tile

    def side_keys(side):
        return keys[:, pl.ds(pl.multiple_of(side * width, width), width)]

    def g_copy(i):
        return remote(g_out.at[i], g_in.at[i], g_send.at[i], g_recv.at[i], peer)

    def send_tile(i, carry):
        lanes = pl.ds(pl.multiple_of(i * tile, tile), tile)
        lse_query = lse_own[:, lanes]
        inner = jnp.zeros((8, tile), jnp.float32)
        for c in range(CHUNKS + 1):
            block = st[i, c]
            weight = jnp.exp2(block - lse_query) + jnp.exp2(block - lse_keys[c].reshape(half, 128))
            if c == CHUNKS:
                key_ids = lax.broadcasted_iota(jnp.int32, block.shape, 0) + f * half
                weight = weight - jnp.where(key_ids == pos_ref[:, lanes], 2.0, 0.0)
            rounded = weight.astype(jnp.bfloat16)
            wt[i, :, c * half : (c + 1) * half] = rounded.T
            inner = inner + jnp.sum(
                (rounded.astype(jnp.float32) * block).reshape(half // 8, 8, tile), 0
            )
        rad[:, lanes] = jnp.sum(inner, 0, keepdims=True)
        g_out[i] = dot(wt[i], side_keys(other)).astype(jnp.bfloat16)
        g_copy(i).start()
        return carry

    lax.fori_loop(0, tiles, send_tile, 0)
    rad_out[0] = rad[...]
    rad_copy = remote(rad_out, rad_in, r_send, r_recv, peer)
    rad_copy.start()

    def keep_tiles(i, carry):
        weights = wt[pl.ds(2 * i, 2)].reshape(2 * tile, wt.shape[-1])
        spot = pl.ds(pl.multiple_of(i * 2 * tile, 2 * tile), 2 * tile)
        grad_ref[spot, :] = dot(weights, side_keys(f))
        return carry

    lax.fori_loop(0, tiles // 2, keep_tiles, 0)
    rad_copy.wait_recv()
    radial = jnp.broadcast_to(LN2 * (rad_out[0] + rad_in[0]), (128, rows)).T
    sharpness = sharp_ref[0, 0]
    for i in range(tiles):
        spot = slice(i * tile, (i + 1) * tile)
        g_copy(i).wait_recv()
        inverse = inv[spot, :1]
        unit = raw[f, spot, :].astype(jnp.float32) * inverse
        whole = (grad_ref[spot, :] + g_in[i].astype(jnp.float32)) * sharpness
        grad_ref[spot, :] = inverse * (whole - unit * radial[spot, :1])

    for i in range(2 * pieces):
        y_copy(i).wait_send()
    for slot in range(GROUP):
        for n in range(STEPS):
            send_key(slot, n).wait_send()
    for j in range(GROUP):
        for h in range(2):
            lse_copy(j, h).wait_send()
    ex_copy.wait_send()
    rad_copy.wait_send()
    for i in range(tiles):
        g_copy(i).wait_send()


def per_device(projected, sharpness, partners, positives):
    rows, width = projected.shape
    blocks = lax.axis_size("tour")
    if blocks != 2 * GROUP or lax.axis_size("feat") != 2:
        return per_device_any(projected, sharpness, partners, positives)
    half = rows // 2
    step_rows = half // CHUNKS
    tiles = rows // 128
    local_pos = (positives - lax.axis_index("tour") * rows)[None, :]
    bf16, f32 = jnp.bfloat16, jnp.float32
    dma = pltpu.SemaphoreType.DMA
    loss, grad = pl.pallas_call(
        functools.partial(kernel, GROUP, rows, width),
        out_shape=(
            jax.ShapeDtypeStruct((1, rows), f32),
            jax.ShapeDtypeStruct((rows, width), f32),
        ),
        in_specs=[
            pl.BlockSpec(memory_space=pltpu.SMEM),
            pl.BlockSpec(memory_space=pl.ANY),
            pl.BlockSpec(memory_space=pltpu.VMEM),
        ],
        out_specs=[pl.BlockSpec(memory_space=pltpu.VMEM)] * 2,
        scratch_shapes=[
            pltpu.VMEM((2, rows, width), bf16),
            pltpu.VMEM((rows, 2 * width), bf16),
            pltpu.VMEM((2 * width, rows), bf16),
            pltpu.VMEM((rows, 128), f32),
            pltpu.VMEM(((CHUNKS + 1) * half, 2 * width), bf16),
            pltpu.VMEM((tiles, CHUNKS + 1, half, 128), f32),
            pltpu.VMEM((tiles, 128, (CHUNKS + 1) * half), bf16),
            pltpu.VMEM((8, rows), f32),
            pltpu.VMEM((8, rows), f32),
            pltpu.VMEM((1, rows), f32),
            pltpu.VMEM((1, rows), f32),
            pltpu.VMEM((4, 1, half), f32),
            pltpu.VMEM((4, 1, half), f32),
            pltpu.VMEM((GROUP, 2, 1, half), f32),
            pltpu.VMEM((128, half), f32),
            pltpu.VMEM((CHUNKS + 1, GROUP, step_rows, 128), f32),
            pltpu.VMEM((tiles, 128, width), bf16),
            pltpu.VMEM((tiles, 128, width), bf16),
            pltpu.VMEM((1, rows), f32),
            pltpu.VMEM((1, 1, rows), f32),
            pltpu.VMEM((1, 1, rows), f32),
            dma, dma((8,)), dma((8,)),
            dma((GROUP, STEPS)), dma((GROUP, STEPS)),
            dma((GROUP, 2)), dma((GROUP, 2)),
            dma, dma,
            dma((tiles,)), dma((tiles,)),
            dma, dma,
        ],
        compiler_params=pltpu.CompilerParams(
            collective_id=0, has_side_effects=True, vmem_limit_bytes=50 * 1024 * 1024
        ),
        cost_estimate=pl.CostEstimate(
            flops=9 * 4 * rows * half * 2 * width, bytes_accessed=4 * rows * width,
            transcendentals=27 * rows * half,
        ),
    )(sharpness.reshape(1, 1), projected, local_pos)
    return loss[0], grad


def solution(mesh):
    in_specs = (P("tour", "feat"), P(), P(), P("tour"))
    out_specs = (P("tour"), P("tour", "feat"))
    return jax.shard_map(
        per_device, mesh=mesh, in_specs=in_specs, out_specs=out_specs, check_vma=False
    )
```
